32 devices in a mesh: section: 16 (over z, x, core), tp: 2 (over y).
Axes of the slice: x: 2, y: 2, z: 4, core: 2. Of those that a mesh axis runs over, the one named last changes fastest.
Arguments:
- fwd_q: bfloat16 [16, 128, 8192], P('section', None, 'tp'), may hold values from -4.5 to 4.5
- fwd_k: bfloat16 [16, 128, 1024], P('section', None, 'tp'), may hold values from -4.5 to 4.5
- fwd_v: bfloat16 [16, 128, 1024], P('section', None, 'tp'), may hold values from -6 to 6
- fwd_segments: int32 [16, 128], P('section'), may hold values from 0 to 3, never falling along the last dimension, each value on 1 to 64 neighbouring positions
- held_q: bfloat16 [16, 128, 8192], P('section', None, 'tp'), may hold values from -4.5 to 4.5
- held_k: bfloat16 [16, 128, 1024], P('section', None, 'tp'), may hold values from -4.5 to 4.5
- held_v: bfloat16 [16, 128, 1024], P('section', None, 'tp'), may hold values from -6 to 6
- back_segments: int32 [16, 128], P('section'), may hold values from 0 to 3, never falling along the last dimension, each value on 1 to 64 neighbouring positions
- up_grad: bfloat16 [16, 128, 8192], P('section', None, 'tp'), may hold values from -6 to 6
Outputs:
- passed_output: bfloat16 [16, 128, 8192], P('section', 'tp')
- evicted_q: bfloat16 [16, 128, 8192], P('section', None, 'tp')
- evicted_k: bfloat16 [16, 128, 1024], P('section', None, 'tp')
- evicted_v: bfloat16 [16, 128, 1024], P('section', None, 'tp')
- grad_q: bfloat16 [16, 128, 8192], P('section', None, 'tp')
- grad_k: bfloat16 [16, 128, 1024], P('section', None, 'tp')
- grad_v: bfloat16 [16, 128, 1024], P('section', None, 'tp')
The draws below stay inside these ranges and needn't reach their ends.
Inputs may be any that keep to these rules, and one draw needn't show every extreme that they name: `fwd_segments`: document numbers never fall along a micro-batch; each document has 1 to 64 tokens. `back_segments`: document numbers never fall along a micro-batch; each document has 1 to 64 tokens.
All inputs are finite; a program needn't handle non-finite values.
Results may differ from the reference program's by a relative error of at most 0.0058.
Values may be sent and summed in bfloat16 or wider, within the bound.
A program may use at most 64 MiB of HBM per device.

```python
import math
import jax
import jax.numpy as jnp
import numpy as np
from jax import lax

HQ = 64
KV = 8
HD = 128
TOKENS = 128
SECTIONS = 16


def query_values(key, fold):
    key = jax.random.fold_in(key, fold)
    values_drawn = jnp.clip(jax.random.normal(key, (SECTIONS, TOKENS, HQ * HD)), -4.5, 4.5)
    return values_drawn.astype(jnp.float32)


def key_values(key, fold):
    key = jax.random.fold_in(key, fold)
    values_drawn = jnp.clip(jax.random.normal(key, (SECTIONS, TOKENS, KV * HD)), -4.5, 4.5)
    return values_drawn.astype(jnp.float32)


def draw_fwd_q(key, part):
    return query_values(key, 1).astype(jnp.bfloat16)


def draw_fwd_k(key, part):
    return key_values(key, 2).astype(jnp.bfloat16)


def draw_held_q(key, part):
    return query_values(key, 3).astype(jnp.bfloat16)


def draw_held_k(key, part):
    return key_values(key, 4).astype(jnp.bfloat16)


def block_scale(key, extent, cuts, low, top_value):
    def one(axis_at, parts):
        steps = jax.random.uniform(jax.random.fold_in(jax.random.fold_in(key, 6), axis_at), (parts,), jnp.float32, low / len(cuts), top_value / len(cuts))
        return jnp.repeat(jnp.exp(steps), extent[axis_at] // parts).reshape((-1,) + (1,) * (len(extent) - axis_at - 1))

    gain = one(*cuts[0])
    for cut in cuts[1:]:
        gain = gain * one(*cut)
    return gain


def split_up(number_of, total, reach, lean):
    loads = [(1 << 20) // math.isqrt(grade ** lean) + 1 for grade in range(2, number_of + 1)]
    rest, counts = total - reach - (number_of - 1), [1] * (number_of - 1)
    while rest > 0:
        candidates = [i for i in range(number_of - 1) if counts[i] < reach]
        whole, budget = sum([loads[i] for i in candidates]), rest
        for i in candidates:
            addition = min(reach - counts[i], max(1, budget * loads[i] // whole), rest)
            counts[i] = counts[i] + addition
            rest = rest - addition
    return np.array([reach] + counts)


def ragged(key, count, total, reach, skew):
    if count == 2:
        one = jax.random.randint(key, (), max(1, total - reach), min(reach, total - 1) + 1)
        return jnp.stack([one, total - one])
    tallies = jnp.asarray(split_up(count, total, reach, skew), jnp.int32)
    pairs = (count - 1) // 2
    donor, taker = tallies[1:1 + 2 * pairs:2], tallies[2:2 + 2 * pairs:2]
    slack = jnp.minimum(donor - 1, reach - taker)
    moved = jax.random.randint(jax.random.fold_in(key, 1), (pairs,), 0, 1 << 20) % (slack + 1)
    tallies = tallies.at[1:1 + 2 * pairs:2].set(donor - moved).at[2:2 + 2 * pairs:2].set(taker + moved)
    return tallies[jax.random.permutation(jax.random.fold_in(key, 2), count)]


def gaussian(key, shape, width, most, pieces=(), kind=jnp.bfloat16):
    array = jax.random.normal(key, shape, jnp.float32) * width
    if len(pieces) > 0:
        array = block_scale(key, shape, pieces, -0.22, 0.18) * array
    return jnp.clip(array, min=-most, max=most).astype(kind)


def setup_inputs(seed: int = 0) -> dict:
    seeds = jax.random.split(jax.random.key(seed), 10)
    fwd_q = draw_fwd_q(jax.random.fold_in(seeds[9], 71), 0)
    fwd_k = draw_fwd_k(jax.random.fold_in(seeds[9], 71), 0)
    fwd_v = gaussian(seeds[2], (SECTIONS, TOKENS, KV * HD), 1.0, 6.0, ((0, 16), (2, 2)))
    fwd_segments = jax.vmap(lambda own: jnp.searchsorted(jnp.cumsum(ragged(own, 4, TOKENS, TOKENS // 2, 2)), jnp.arange(TOKENS), side="right"))(jax.random.split(seeds[3], SECTIONS)).reshape((SECTIONS, TOKENS)).astype(jnp.int32)
    held_q = draw_held_q(jax.random.fold_in(seeds[9], 71), 0)
    held_k = draw_held_k(jax.random.fold_in(seeds[9], 71), 0)
    held_v = gaussian(seeds[6], (SECTIONS, TOKENS, KV * HD), 1.0, 6.0, ((0, 16), (2, 2)))
    back_segments = jax.vmap(lambda own: jnp.searchsorted(jnp.cumsum(ragged(own, 4, TOKENS, TOKENS // 2, 2)), jnp.arange(TOKENS), side="right"))(jax.random.split(seeds[7], SECTIONS)).reshape((SECTIONS, TOKENS)).astype(jnp.int32)
    up_grad = gaussian(seeds[8], (SECTIONS, TOKENS, HQ * HD), 1.0, 6.0, ((0, 16), (2, 2)))
    return {"fwd_q": fwd_q, "fwd_k": fwd_k, "fwd_v": fwd_v, "fwd_segments": fwd_segments, "held_q": held_q, "held_k": held_k, "held_v": held_v, "back_segments": back_segments, "up_grad": up_grad}


def probability(query_heads, key_heads, segment_ids):
    row_count = query_heads.shape[0]
    scores = jnp.einsum("qkgd,skd->kgqs", query_heads, key_heads) * (HD ** -0.5)
    positions = jnp.arange(row_count)
    allowed = (segment_ids[:, None] == segment_ids[None, :]) & (positions[:, None] >= positions[None, :])
    scores = jnp.where(allowed, scores, -jnp.inf)
    row_max = jnp.max(scores, axis=-1, keepdims=True)
    weights = jnp.exp(scores - row_max)
    return weights / jnp.sum(weights, axis=-1, keepdims=True)


def split_heads(queries, key_rows, value_rows):
    row_count = queries.shape[0]
    group_size = HQ // KV
    query_heads = queries.astype(jnp.float32).reshape(row_count, KV, group_size, HD)
    key_heads = key_rows.astype(jnp.float32).reshape(row_count, KV, HD)
    value_heads = value_rows.astype(jnp.float32).reshape(row_count, KV, HD)
    return query_heads, key_heads, value_heads


def forward(queries, key_rows, value_rows, segment_ids):
    query_heads, key_heads, value_heads = split_heads(queries, key_rows, value_rows)
    prob = probability(query_heads, key_heads, segment_ids)
    prob_low = lax.optimization_barrier(prob.astype(jnp.bfloat16)).astype(jnp.float32)
    result = jnp.einsum("kgqs,skd->qkgd", prob_low, value_heads)
    return result.reshape(queries.shape[0], HQ * HD).astype(jnp.bfloat16)


def backward(queries, key_rows, value_rows, segment_ids, out_grad):
    row_count = queries.shape[0]
    query_heads, key_heads, value_heads = split_heads(queries, key_rows, value_rows)
    prob = probability(query_heads, key_heads, segment_ids)
    prob_low = lax.optimization_barrier(prob.astype(jnp.bfloat16)).astype(jnp.float32)
    grad_heads = out_grad.astype(jnp.float32).reshape(row_count, KV, HQ // KV, HD)
    value_grad = jnp.einsum("kgqs,qkgd->skd", prob_low, grad_heads)
    dprob = jnp.einsum("qkgd,skd->kgqs", grad_heads, value_heads)
    delta = jnp.sum(prob * dprob, axis=-1, keepdims=True)
    dscore = prob * (dprob - delta) * (HD ** -0.5)
    dscore = lax.optimization_barrier(dscore.astype(jnp.bfloat16)).astype(jnp.float32)
    query_grad = jnp.einsum("kgqs,skd->qkgd", dscore, key_heads)
    key_grad = jnp.einsum("kgqs,qkgd->skd", dscore, query_heads)
    return (query_grad.reshape(row_count, HQ * HD).astype(jnp.bfloat16),
            key_grad.reshape(row_count, KV * HD).astype(jnp.bfloat16),
            value_grad.reshape(row_count, KV * HD).astype(jnp.bfloat16))


def reference(fwd_q, fwd_k, fwd_v, fwd_segments, held_q, held_k, held_v, back_segments, up_grad):
    outputs = lax.map(lambda items: forward(*items), (fwd_q, fwd_k, fwd_v, fwd_segments))
    passed_output = jnp.roll(outputs, 1, axis=0)
    evicted_q = jnp.flip(fwd_q, axis=0)
    evicted_k = jnp.flip(fwd_k, axis=0)
    evicted_v = jnp.flip(fwd_v, axis=0)
    own_q = jnp.flip(held_q, axis=0)
    own_k = jnp.flip(held_k, axis=0)
    own_v = jnp.flip(held_v, axis=0)
    arriving = jnp.roll(up_grad, -1, axis=0)
    grad_q, grad_k, grad_v = lax.map(lambda items: backward(*items), (own_q, own_k, own_v, back_segments, arriving))
    return passed_output, evicted_q, evicted_k, evicted_v, grad_q, grad_k, grad_v
```

```python
import jax
import jax.numpy as jnp
from jax import lax
from jax.sharding import PartitionSpec as P

HQ = 64
KV = 8
HD = 128


def split_heads(queries, key_rows, value_rows):
    row_count = queries.shape[0]
    kv_local = key_rows.shape[1] // HD
    group_size = HQ // KV
    query_heads = queries.reshape(row_count, kv_local, group_size, HD)
    key_heads = key_rows.reshape(row_count, kv_local, HD)
    value_heads = value_rows.reshape(row_count, kv_local, HD)
    return (query_heads, key_heads, value_heads)


def probability(query_heads, key_heads, segment_ids):
    row_count = query_heads.shape[0]
    scores = jnp.einsum(
        "qkgd,skd->kgqs", query_heads, key_heads, preferred_element_type=jnp.float32
    ) * HD ** (-0.5)
    positions = jnp.arange(row_count)
    allowed = (segment_ids[:, None] == segment_ids[None, :]) & (
        positions[:, None] >= positions[None, :]
    )
    scores = jnp.where(allowed, scores, -jnp.inf)
    row_max = jnp.max(scores, axis=-1, keepdims=True)
    weights = jnp.exp(scores - row_max)
    return weights / jnp.sum(weights, axis=-1, keepdims=True)


def forward(queries, key_rows, value_rows, segment_ids):
    query_heads, key_heads, value_heads = split_heads(queries, key_rows, value_rows)
    prob = probability(query_heads, key_heads, segment_ids)
    prob_low = prob.astype(jnp.bfloat16)
    result = jnp.einsum("kgqs,skd->qkgd", prob_low, value_heads, preferred_element_type=jnp.float32)
    return result.reshape(queries.shape[0], queries.shape[1]).astype(jnp.bfloat16)


def backward(queries, key_rows, value_rows, segment_ids, out_grad):
    row_count = queries.shape[0]
    query_heads, key_heads, value_heads = split_heads(queries, key_rows, value_rows)
    prob = probability(query_heads, key_heads, segment_ids)
    prob_low = prob.astype(jnp.bfloat16)
    grad_heads = out_grad.reshape(query_heads.shape)
    value_grad = jnp.einsum(
        "kgqs,qkgd->skd", prob_low, grad_heads, preferred_element_type=jnp.float32
    )
    dprob = jnp.einsum(
        "qkgd,skd->kgqs", grad_heads, value_heads, preferred_element_type=jnp.float32
    )
    delta = jnp.sum(prob * dprob, axis=-1, keepdims=True)
    dscore = (prob * (dprob - delta) * HD ** (-0.5)).astype(jnp.bfloat16)
    query_grad = jnp.einsum("kgqs,skd->qkgd", dscore, key_heads, preferred_element_type=jnp.float32)
    key_grad = jnp.einsum("kgqs,qkgd->skd", dscore, query_heads, preferred_element_type=jnp.float32)
    return (
        query_grad.reshape(row_count, queries.shape[1]).astype(jnp.bfloat16),
        key_grad.reshape(row_count, key_rows.shape[1]).astype(jnp.bfloat16),
        value_grad.reshape(row_count, key_rows.shape[1]).astype(jnp.bfloat16),
    )


def mirrored(value):
    count = lax.axis_size("section")
    return lax.ppermute(value, "section", [(j, count - 1 - j) for j in range(count)])


def passed_on(out_local):
    sections, splits = lax.axis_size("section"), lax.axis_size("tp")
    own = lax.axis_index("tp")
    rows, width = out_local.shape[0] // splits, out_local.shape[1]
    passed = jnp.zeros((rows, splits, width), out_local.dtype)
    for offset in range(splits):
        piece = lax.dynamic_slice_in_dim(out_local, lax.rem(own + offset, splits) * rows, rows, 0)
        pairs = [
            (s * splits + t, (s + 1) % sections * splits + (t + offset) % splits)
            for s in range(sections)
            for t in range(splits)
        ]
        piece = lax.ppermute(piece, ("section", "tp"), pairs)
        came_from = lax.rem(own - offset + splits, splits)
        passed = lax.dynamic_update_slice_in_dim(passed, piece[:, None], came_from, 1)
    return passed.reshape(rows, splits * width)


def shards(fwd_q, fwd_k, fwd_v, fwd_segments, held_q, held_k, held_v, back_segments, up_grad):
    sections = lax.axis_size("section")
    own_k = mirrored(held_k[0])
    own_q = mirrored(held_q[0])
    own_v = mirrored(held_v[0])
    arriving = lax.ppermute(up_grad[0], "section", [(j, (j - 1) % sections) for j in range(sections)])
    out_local = forward(fwd_q[0], fwd_k[0], fwd_v[0], fwd_segments[0])
    passed_output = passed_on(out_local)
    evicted_q = mirrored(fwd_q[0])
    evicted_k = mirrored(fwd_k[0])
    evicted_v = mirrored(fwd_v[0])
    grad_q, grad_k, grad_v = backward(own_q, own_k, own_v, back_segments[0], arriving)
    return (
        passed_output[None],
        evicted_q[None],
        evicted_k[None],
        evicted_v[None],
        grad_q[None],
        grad_k[None],
        grad_v[None],
    )


def solution(mesh):
    heads = P("section", None, "tp")
    tokens = P("section", None)
    return jax.shard_map(
        shards,
        mesh=mesh,
        in_specs=(heads, heads, heads, tokens, heads, heads, heads, tokens, heads),
        out_specs=(P("section", "tp", None),) + (heads,) * 6,
        check_vma=False,
    )
```

```python
import functools

import jax
import jax.numpy as jnp
from jax import lax
from jax.experimental import pallas as pl
from jax.experimental.pallas import tpu as pltpu
from jax.sharding import PartitionSpec as P

HQ = 64
KV = 8
HD = 128
GROUP = HQ // KV
SCALE = HD**-0.5
LOW = jnp.bfloat16
F32 = jnp.float32
DIAG_ROWS = 16


def dot_nt(a, b):
    return lax.dot_general(a, b, (((1,), (1,)), ((), ())), preferred_element_type=F32)


def dot_tn(a, b):
    return lax.dot_general(a, b, (((0,), (0,)), ((), ())), preferred_element_type=F32)


def dot_nn(a, b):
    return lax.dot_general(a, b, (((1,), (0,)), ((), ())), preferred_element_type=F32)


def iotas(shape):
    return lax.broadcasted_iota(jnp.int32, shape, 0), lax.broadcasted_iota(jnp.int32, shape, 1)


def allowed_mask(seg_col, seg_row):
    tokens = seg_row.shape[1]
    rows, cols = iotas((tokens, tokens))
    return (seg_col == seg_row) & (cols <= rows)


def probability(q, k, allowed):
    scores = jnp.where(allowed, dot_nt(q, k) * SCALE, -jnp.inf)
    weights = jnp.exp(scores - jnp.max(scores, axis=1, keepdims=True))
    return weights / jnp.sum(weights, axis=1, keepdims=True)


def pack(full):
    half = full.shape[0] // 2
    rows, cols = iotas((half, half))
    turned = full[half:, :].T
    packed = full[:half, :half] + turned[:half] + jnp.where(rows < cols, turned[half:], 0.0)
    diag = jnp.sum(jnp.where(rows == cols, full[half:, half:], 0.0), axis=0, keepdims=True)
    return packed, diag


def unpack_masks(seg_col, seg_row):
    half = seg_row.shape[1] // 2
    rows, cols = iotas((half, half))
    first = (seg_col[:half] == seg_row[:, :half]) & (cols <= rows)
    cross = seg_col[:half] == seg_row[:, half:]
    second = (seg_col[half:] == seg_row[:, half:]) & (rows < cols)
    return first, jnp.concatenate([cross, second], axis=0), rows == cols


def unpack(packed, diag, masks):
    first, turned_mask, eye = masks
    turned = jnp.where(turned_mask, jnp.concatenate([packed, packed], axis=0), 0.0).T
    half = packed.shape[0]
    zero = jnp.zeros((half, half), F32)
    on_diag = jnp.where(eye, jnp.broadcast_to(diag, (half, half)), 0.0)
    top = jnp.concatenate([jnp.where(first, packed, 0.0), zero], axis=1)
    bottom = turned + jnp.concatenate([zero, on_diag], axis=1)
    return jnp.concatenate([top, bottom], axis=0)


def store_packed(g, kv_local, parts, diag_scratch, pack_ref):
    half = parts[0][0].shape[0]
    values = jnp.concatenate([p for p, _ in parts], axis=1).astype(LOW)
    pack_ref[pl.ds(pl.multiple_of(g * half, half), half), :] = values
    diags = jnp.concatenate([d for _, d in parts], axis=1)
    rows, _ = iotas(diag_scratch.shape)
    merged = jnp.where(rows == g, jnp.broadcast_to(diags, rows.shape), diag_scratch[...])
    diag_scratch[...] = merged

    @pl.when(g == kv_local - 1)
    def _():
        pack_ref[pl.ds(kv_local * half, DIAG_ROWS), :] = jnp.where(rows < kv_local, merged, 0.0).astype(LOW)


def load_packed(g, kv_local, pack_ref):
    half = (pack_ref.shape[0] - DIAG_ROWS) // kv_local
    values = pack_ref[pl.ds(pl.multiple_of(g * half, half), half), :].astype(F32)
    tail = pack_ref[pl.ds(kv_local * half, DIAG_ROWS), :].astype(F32)
    rows, _ = iotas(tail.shape)
    diags = jnp.sum(jnp.where(rows == g, tail, 0.0), axis=0, keepdims=True)
    return [
        (values[:, h * half : (h + 1) * half], diags[:, h * half : (h + 1) * half]) for h in range(GROUP)
    ]


def head(h):
    return slice(h * HD, (h + 1) * HD)


def forward_body(q_ref, k_ref, v_ref, seg_col, seg_row, out_ref):
    allowed = allowed_mask(seg_col[...], seg_row[...])
    k, v = k_ref[...], v_ref[...]
    for h in range(GROUP):
        prob = probability(q_ref[:, head(h)], k, allowed)
        out_ref[:, head(h)] = dot_nn(prob.astype(LOW), v).astype(LOW)


def score_gradient(prob, grad, v):
    dprob = dot_nt(grad, v)
    delta = jnp.sum(prob * dprob, axis=1, keepdims=True)
    return prob * (dprob - delta) * SCALE


def holder_body(kv_local, special, q_ref, k_ref, v_ref, grad_ref, seg_col, seg_row, pack_ref, third_ref, diag_scratch):
    g = pl.program_id(0)
    allowed = allowed_mask(seg_col[...], seg_row[...])
    k = k_ref[...]

    @pl.when(special[0] == 0)
    def _():
        parts = [pack(probability(q_ref[:, head(h)], k, allowed)) for h in range(GROUP)]
        store_packed(g, kv_local, parts, diag_scratch, pack_ref)
        third_ref[...] = v_ref[...]

    @pl.when(special[0] != 0)
    def _():
        v = v_ref[...]
        parts = []
        total = jnp.zeros(third_ref.shape, F32)
        for h in range(GROUP):
            prob = probability(q_ref[:, head(h)], k, allowed)
            grad = grad_ref[:, head(h)]
            total = total + dot_tn(prob.astype(LOW), grad)
            parts.append(pack(score_gradient(prob, grad, v)))
        store_packed(g, kv_local, parts, diag_scratch, pack_ref)
        third_ref[...] = total.astype(LOW)


def section_body(kv_local, special, in_ref, k_ref, third_ref, grad_ref, seg_col, seg_row, pack_ref, gq_ref, gv_ref, diag_scratch):
    g = pl.program_id(0)
    masks = unpack_masks(seg_col[...], seg_row[...])
    k = k_ref[...]

    @pl.when(special[0] == 0)
    def _():
        v = third_ref[...]
        parts = []
        total = jnp.zeros(gv_ref.shape, F32)
        for h, (packed, diag) in enumerate(load_packed(g, kv_local, in_ref)):
            prob = unpack(packed, diag, masks)
            grad = grad_ref[:, head(h)]
            total = total + dot_tn(prob.astype(LOW), grad)
            dscore = score_gradient(prob, grad, v)
            gq_ref[:, head(h)] = dot_nn(dscore.astype(LOW), k).astype(LOW)
            parts.append(pack(dscore))
        store_packed(g, kv_local, parts, diag_scratch, pack_ref)
        gv_ref[...] = total.astype(LOW)

    @pl.when(special[0] != 0)
    def _():
        pack_ref[...] = in_ref[...]
        gv_ref[...] = third_ref[...]
        for h, (packed, diag) in enumerate(load_packed(g, kv_local, in_ref)):
            dscore = unpack(packed, diag, masks)
            gq_ref[:, head(h)] = dot_nn(dscore.astype(LOW), k).astype(LOW)


def key_body(kv_local, pack_ref, q_ref, seg_col, seg_row, gk_ref):
    g = pl.program_id(0)
    masks = unpack_masks(seg_col[...], seg_row[...])
    total = jnp.zeros(gk_ref.shape, F32)
    for h, (packed, diag) in enumerate(load_packed(g, kv_local, pack_ref)):
        dscore = unpack(packed, diag, masks).astype(LOW)
        total = total + dot_tn(dscore, q_ref[:, head(h)])
    gk_ref[...] = total.astype(LOW)


def specs(tokens):
    wide = pl.BlockSpec((tokens, GROUP * HD), lambda g: (0, g))
    narrow = pl.BlockSpec((tokens, HD), lambda g: (0, g))
    seg = [pl.BlockSpec((tokens, 1), lambda g: (0, 0)), pl.BlockSpec((1, tokens), lambda g: (0, 0))]
    return wide, narrow, seg


def run(body, kv_local, in_specs, out_specs, out_shape, scratch, gflop, args):
    return pl.pallas_call(
        body,
        grid=(kv_local,),
        in_specs=in_specs,
        out_specs=out_specs,
        out_shape=out_shape,
        scratch_shapes=scratch,
        compiler_params=pltpu.CompilerParams(vmem_limit_bytes=24 * 2**20),
        cost_estimate=pl.CostEstimate(flops=int(gflop * 2**30), bytes_accessed=2**22, transcendentals=0),
    )(*args)


def mirrored(value):
    count = lax.axis_size("section")
    return lax.ppermute(value, "section", [(j, count - 1 - j) for j in range(count)])


def passed_on(out_local):
    sections, splits = lax.axis_size("section"), lax.axis_size("tp")
    own = lax.axis_index("tp")
    rows, width = out_local.shape[0] // splits, out_local.shape[1]
    came = []
    for offset in range(splits):
        piece = lax.dynamic_slice_in_dim(out_local, lax.rem(own + offset, splits) * rows, rows, 0)
        pairs = [
            (s * splits + t, (s + 1) % sections * splits + (t + offset) % splits)
            for s in range(sections)
            for t in range(splits)
        ]
        came.append(lax.ppermute(piece, ("section", "tp"), pairs))
    blocks = []
    for place in range(splits):
        offset = lax.rem(own - place + splits, splits)
        blocks.append(lax.select_n(offset, *came) if splits > 2 else jnp.where(offset == 0, came[0], came[-1]))
    return jnp.concatenate(blocks, axis=1)


def shards(fwd_q, fwd_k, fwd_v, fwd_segments, held_q, held_k, held_v, back_segments, up_grad):
    sections = lax.axis_size("section")
    me = lax.axis_index("section")
    tokens, half = held_q.shape[1], held_q.shape[1] // 2
    kv_local = held_k.shape[2] // HD
    wide, narrow, seg = specs(tokens)
    smem = pl.BlockSpec(memory_space=pltpu.SMEM)
    pack_shape = (kv_local * half + DIAG_ROWS, GROUP * half)
    whole = pl.BlockSpec(pack_shape, lambda g: (0, 0))
    packed_type = jax.ShapeDtypeStruct(pack_shape, LOW)
    wide_type = jax.ShapeDtypeStruct(held_q.shape[1:], LOW)
    narrow_type = jax.ShapeDtypeStruct(held_k.shape[1:], LOW)
    diag_scratch = [pltpu.VMEM((DIAG_ROWS, GROUP * half), F32)]

    def columns(ids):
        return ids.reshape(tokens, 1), ids.reshape(1, tokens)

    shortcuts = [i for i in range(sections) if (i + 1) % sections == sections - 1 - i]
    section_special = sum([(me == i).astype(jnp.int32) for i in shortcuts]).reshape(1)
    holder_special = sum([(me == sections - 1 - i).astype(jnp.int32) for i in shortcuts]).reshape(1)

    held_ids = mirrored(back_segments[0])
    evicted_k = mirrored(fwd_k[0])
    evicted_v = mirrored(fwd_v[0])
    evicted_q = mirrored(fwd_q[0])
    keys = mirrored(held_k[0])
    arriving = lax.ppermute(
        up_grad[0],
        "section",
        [((i + 1) % sections, i) for i in range(sections) if i not in shortcuts],
    )
    packed, third = run(
        functools.partial(holder_body, kv_local),
        kv_local,
        [smem, wide, narrow, narrow, wide] + seg,
        [whole, narrow],
        [packed_type, narrow_type],
        diag_scratch,
        0.3,
        (holder_special, held_q[0], held_k[0], held_v[0], up_grad[0]) + columns(held_ids),
    )
    packed_here, third_here = mirrored(packed), mirrored(third)
    out_local = run(
        forward_body,
        kv_local,
        [wide, narrow, narrow] + seg,
        wide,
        wide_type,
        [],
        0.3,
        (fwd_q[0], fwd_k[0], fwd_v[0]) + columns(fwd_segments[0]),
    )
    passed_output = passed_on(out_local)
    dscore, grad_q, grad_v = run(
        functools.partial(section_body, kv_local),
        kv_local,
        [smem, whole, narrow, narrow, wide] + seg,
        [whole, wide, narrow],
        [packed_type, wide_type, narrow_type],
        diag_scratch,
        0.5,
        (section_special, packed_here, keys, third_here, arriving) + columns(back_segments[0]),
    )
    dscore_back = lax.ppermute(
        dscore, "section", [(i, sections - 1 - i) for i in range(sections) if i not in shortcuts]
    )
    dscore_held = jnp.where(holder_special[0] != 0, packed, dscore_back)
    grad_k = run(
        functools.partial(key_body, kv_local),
        kv_local,
        [whole, wide] + seg,
        narrow,
        narrow_type,
        [],
        0.2,
        (dscore_held, held_q[0]) + columns(held_ids),
    )
    grad_k = mirrored(grad_k)
    return (
        passed_output[None],
        evicted_q[None],
        evicted_k[None],
        evicted_v[None],
        grad_q[None],
        grad_k[None],
        grad_v[None],
    )


def solution(mesh):
    heads = P("section", None, "tp")
    tokens = P("section", None)
    return jax.shard_map(
        shards,
        mesh=mesh,
        in_specs=(heads, heads, heads, tokens, heads, heads, heads, tokens, heads),
        out_specs=(P("section", "tp", None),) + (heads,) * 6,
        check_vma=False,
    )
```

```python
import functools

import jax
import jax.numpy as jnp
from jax import lax
from jax.experimental import pallas as pl
from jax.experimental.pallas import tpu as pltpu
from jax.sharding import PartitionSpec as P

HQ = 64
KV = 8
HD = 128
GROUP = HQ // KV
SCALE = HD**-0.5
LOW = jnp.bfloat16
F32 = jnp.float32
DIAG_ROWS = 16
MESH = pl.DeviceIdType.MESH


def dot_nt(a, b):
    return lax.dot_general(a, b, (((1,), (1,)), ((), ())), preferred_element_type=F32)


def dot_tn(a, b):
    return lax.dot_general(a, b, (((0,), (0,)), ((), ())), preferred_element_type=F32)


def dot_nn(a, b):
    return lax.dot_general(a, b, (((1,), (0,)), ((), ())), preferred_element_type=F32)


def iotas(shape):
    return lax.broadcasted_iota(jnp.int32, shape, 0), lax.broadcasted_iota(jnp.int32, shape, 1)


def segment_sides(ids_ref):
    tokens = ids_ref.shape[1]
    across = jnp.broadcast_to(ids_ref[...].astype(F32), (tokens, tokens))
    return across.T, across


def allowed_mask(down, across):
    rows, cols = iotas(down.shape)
    return (down == across) & (cols <= rows)


def probability(q, k, allowed):
    scores = jnp.where(allowed, dot_nt(q, k) * SCALE, -jnp.inf)
    weights = jnp.exp(scores - jnp.max(scores, axis=1, keepdims=True))
    return weights / jnp.sum(weights, axis=1, keepdims=True)


def pack(full):
    half = full.shape[0] // 2
    rows, cols = iotas((half, half))
    turned = full[half:, :].T
    packed = full[:half, :half] + turned[:half] + jnp.where(rows < cols, turned[half:], 0.0)
    diag = jnp.sum(jnp.where(rows == cols, full[half:, half:], 0.0), axis=0, keepdims=True)
    return packed, diag


def unpack_masks(down, across):
    half = down.shape[0] // 2
    rows, cols = iotas((half, half))
    first = (down[:half, :half] == across[:half, :half]) & (cols <= rows)
    cross = down[:half, :half] == across[:half, half:]
    second = (down[half:, half:] == across[half:, half:]) & (rows < cols)
    return first, jnp.concatenate([cross, second], axis=0), rows == cols


def unpack(packed, diag, masks):
    first, turned_mask, eye = masks
    turned = jnp.where(turned_mask, jnp.concatenate([packed, packed], axis=0), 0.0).T
    half = packed.shape[0]
    zero = jnp.zeros((half, half), F32)
    on_diag = jnp.where(eye, jnp.broadcast_to(diag, (half, half)), 0.0)
    top = jnp.concatenate([jnp.where(first, packed, 0.0), zero], axis=1)
    bottom = turned + jnp.concatenate([zero, on_diag], axis=1)
    return jnp.concatenate([top, bottom], axis=0)


def store_packed(g, parts, diag_scratch, pack_ref):
    half = parts[0][0].shape[0]
    values = jnp.concatenate([p for p, _ in parts], axis=1).astype(LOW)
    pack_ref[pl.ds(pl.multiple_of(g * half, half), half), :] = values
    diags = jnp.concatenate([d for _, d in parts], axis=1)
    rows, _ = iotas(diag_scratch.shape)
    diag_scratch[...] = jnp.where(rows == g, jnp.broadcast_to(diags, rows.shape), diag_scratch[...])


def load_packed(g, pack_ref):
    half = pack_ref.shape[1] // GROUP
    values = pack_ref[pl.ds(pl.multiple_of(g * half, half), half), :].astype(F32)
    tail = pack_ref[pl.ds(pack_ref.shape[0] - DIAG_ROWS, DIAG_ROWS), :].astype(F32)
    rows, _ = iotas(tail.shape)
    diags = jnp.sum(jnp.where(rows == g, tail, 0.0), axis=0, keepdims=True)
    return [
        (values[:, h * half : (h + 1) * half], diags[:, h * half : (h + 1) * half]) for h in range(GROUP)
    ]


def head(g, h):
    return pl.ds(pl.multiple_of((g * GROUP + h) * HD, HD), HD)


def own(g):
    return pl.ds(pl.multiple_of(g * HD, HD), HD)


def score_gradient(prob, grad, v):
    dprob = dot_nt(grad, v)
    delta = jnp.sum(prob * dprob, axis=1, keepdims=True)
    return prob * (dprob - delta) * SCALE


def every_group(kv_local, body):
    lax.fori_loop(0, kv_local, lambda g, carry: (body(g), carry)[1], 0)


def tick(
    sections, splits,
    fwd_q, fwd_k, fwd_v, fwd_ids, held_q, held_k, held_v, back_ids, up_grad,
    passed, evicted_q, evicted_k, evicted_v, grad_q, grad_k, grad_v,
    fq, fk, fv, fids, hq, hk, hv, bids, ug,
    out, holder_ids, keys, third, third_in, arriving, pack_out, pack_in, score_out, score_in, gk, diag,
    load_sem, send_sem, recv_sem, out_send, out_recv,
):
    me, lane = lax.axis_index("section"), lax.axis_index("tp")
    mirror = sections - 1 - me
    right, left = lax.rem(me + 1, sections), lax.rem(me + sections - 1, sections)
    section_short = right == mirror
    holder_short = lax.rem(mirror + 1, sections) == me
    tokens = hq.shape[0]
    kv_local = hk.shape[1] // HD
    rows = tokens // splits
    width = hq.shape[1]

    pairs = [(held_q, hq), (held_k, hk), (held_v, hv), (up_grad, ug), (fwd_q, fq), (fwd_k, fk), (fwd_v, fv),
             (fwd_ids, fids), (back_ids, bids)]
    loads = [pltpu.make_async_copy(src, dst, load_sem.at[n]) for n, (src, dst) in enumerate(pairs)]
    for load in loads:
        load.start()

    barrier = pltpu.get_barrier_semaphore()
    pl.semaphore_signal(barrier, inc=1, device_id=(mirror, lane), device_id_type=MESH)
    for t in range(splits):
        pl.semaphore_signal(barrier, inc=1, device_id=(left, t), device_id_type=MESH)
        pl.semaphore_signal(barrier, inc=1, device_id=(right, t), device_id_type=MESH)
    pl.semaphore_wait(barrier, 1 + 2 * splits)

    def remote(n, src, dst, section):
        return pltpu.make_async_remote_copy(
            src_ref=src, dst_ref=dst, send_sem=send_sem.at[n], recv_sem=recv_sem.at[n],
            device_id=(section, lane), device_id_type=MESH,
        )

    chunk = tokens // 4
    send_ids = remote(0, back_ids, holder_ids, mirror)
    send_keys = remote(1, held_k, keys, mirror)
    send_ek = remote(2, fwd_k, evicted_k, mirror)
    send_ev = remote(3, fwd_v, evicted_v, mirror)
    send_pack = remote(4, pack_out, pack_in, mirror)
    send_third = remote(5, third, third_in, mirror)
    send_score = remote(6, score_out, score_in, mirror)
    send_gk = remote(7, gk, grad_k, mirror)
    send_up = remote(8, up_grad, arriving, left)
    send_eq = [
        remote(9 + c, fwd_q.at[pl.ds(c * chunk, chunk)], evicted_q.at[pl.ds(c * chunk, chunk)], mirror)
        for c in range(4)
    ]
    send_out = []
    for offset in range(splits):
        to = lax.rem(lane + offset, splits)
        send_out.append(
            pltpu.make_async_remote_copy(
                src_ref=out.at[pl.ds(pl.multiple_of(to * rows, rows), rows)],
                dst_ref=passed.at[:, pl.ds(pl.multiple_of(lane * width, width), width)],
                send_sem=out_send.at[offset], recv_sem=out_recv.at[offset],
                device_id=(right, to), device_id_type=MESH,
            )
        )

    send_ids.start()
    send_keys.start()
    send_ek.start()

    @pl.when(jnp.logical_not(holder_short))
    def _():
        send_up.start()

    diag[...] = jnp.zeros(diag.shape, F32)

    def close_pack(ref):
        ref[pl.ds(ref.shape[0] - DIAG_ROWS, DIAG_ROWS), :] = diag[...].astype(LOW)

    for load in loads[:4]:
        load.wait()
    send_ids.wait_recv()

    @pl.when(jnp.logical_not(holder_short))
    def _():
        allowed = allowed_mask(*segment_sides(holder_ids))

        def group(g):
            k = hk[:, own(g)]
            parts = [pack(probability(hq[:, head(g, h)], k, allowed)) for h in range(GROUP)]
            store_packed(g, parts, diag, pack_out)

        every_group(kv_local, group)
        third[...] = hv[...]

    @pl.when(holder_short)
    def _():
        allowed = allowed_mask(*segment_sides(holder_ids))

        def group(g):
            k, v = hk[:, own(g)], hv[:, own(g)]
            total = jnp.zeros((tokens, HD), F32)
            parts = []
            for h in range(GROUP):
                prob = probability(hq[:, head(g, h)], k, allowed)
                grad = ug[:, head(g, h)]
                total = total + dot_tn(prob.astype(LOW), grad)
                parts.append(pack(score_gradient(prob, grad, v)))
            store_packed(g, parts, diag, pack_out)
            third[:, own(g)] = total.astype(LOW)

        every_group(kv_local, group)

    close_pack(pack_out)
    send_pack.start()
    send_third.start()
    send_ev.start()
    send_eq[0].start()
    send_eq[1].start()

    for load in loads[4:]:
        load.wait()
    forward_allowed = allowed_mask(*segment_sides(fids))

    def forward_group(g):
        k, v = fk[:, own(g)], fv[:, own(g)]
        for h in range(GROUP):
            prob = probability(fq[:, head(g, h)], k, forward_allowed)
            out[:, head(g, h)] = dot_nn(prob.astype(LOW), v).astype(LOW)

    every_group(kv_local, forward_group)
    for send in send_out:
        send.start()

    send_keys.wait_recv()
    send_pack.wait_recv()
    send_third.wait_recv()
    masks = unpack_masks(*segment_sides(bids))

    @pl.when(jnp.logical_not(section_short))
    def _():
        send_up.wait_recv()

        def group(g):
            k, v = keys[:, own(g)], third_in[:, own(g)]
            total = jnp.zeros((tokens, HD), F32)
            parts = []
            for h, (packed, on_diag) in enumerate(load_packed(g, pack_in)):
                prob = unpack(packed, on_diag, masks)
                grad = arriving[:, head(g, h)]
                total = total + dot_tn(prob.astype(LOW), grad)
                dscore = score_gradient(prob, grad, v)
                grad_q[:, head(g, h)] = dot_nn(dscore.astype(LOW), k).astype(LOW)
                parts.append(pack(dscore))
            store_packed(g, parts, diag, score_out)
            grad_v[:, own(g)] = total.astype(LOW)

        every_group(kv_local, group)
        close_pack(score_out)
        send_score.start()

    send_eq[2].start()

    @pl.when(section_short)
    def _():
        def group(g):
            k = keys[:, own(g)]
            for h, (packed, on_diag) in enumerate(load_packed(g, pack_in)):
                dscore = unpack(packed, on_diag, masks)
                grad_q[:, head(g, h)] = dot_nn(dscore.astype(LOW), k).astype(LOW)

        every_group(kv_local, group)
        grad_v[...] = third_in[...]

    def key_gradient(ref):
        holder_masks = unpack_masks(*segment_sides(holder_ids))

        def group(g):
            total = jnp.zeros((tokens, HD), F32)
            for h, (packed, on_diag) in enumerate(load_packed(g, ref)):
                dscore = unpack(packed, on_diag, holder_masks).astype(LOW)
                total = total + dot_tn(dscore, hq[:, head(g, h)])
            gk[:, own(g)] = total.astype(LOW)

        every_group(kv_local, group)

    @pl.when(holder_short)
    def _():
        key_gradient(pack_out)

    @pl.when(jnp.logical_not(holder_short))
    def _():
        send_score.wait_recv()
        key_gradient(score_in)

    send_gk.start()
    send_eq[3].start()

    for send in [send_ids, send_keys, send_ek, send_ev, send_pack, send_third, send_gk] + send_eq + send_out:
        send.wait_send()

    @pl.when(jnp.logical_not(holder_short))
    def _():
        send_up.wait_send()

    @pl.when(jnp.logical_not(section_short))
    def _():
        send_score.wait_send()

    for send in [send_ek, send_ev, send_gk] + send_eq + send_out:
        send.wait_recv()


def shards(fwd_q, fwd_k, fwd_v, fwd_segments, held_q, held_k, held_v, back_segments, up_grad):
    sections, splits = lax.axis_size("section"), lax.axis_size("tp")
    tokens, width = held_q.shape[1], held_q.shape[2]
    narrow_width = held_k.shape[2]
    kv_local = narrow_width // HD
    wide, narrow, ids = (tokens, width), (tokens, narrow_width), (1, tokens)
    packed = (kv_local * (tokens // 2) + DIAG_ROWS, GROUP * (tokens // 2))
    passed = (tokens // splits, splits * width)
    anywhere, vmem = pl.BlockSpec(memory_space=pl.ANY), pl.BlockSpec(memory_space=pltpu.VMEM)

    def low(*shapes):
        return [pltpu.VMEM(shape, LOW) for shape in shapes]

    def number(*shapes):
        return [pltpu.VMEM(shape, jnp.int32) for shape in shapes]

    results = pl.pallas_call(
        functools.partial(tick, sections, splits),
        in_specs=[anywhere] * 9,
        out_specs=[anywhere] * 4 + [vmem, anywhere, vmem],
        out_shape=[jax.ShapeDtypeStruct(s, LOW) for s in (passed, wide, narrow, narrow, wide, narrow, narrow)],
        scratch_shapes=low(wide, narrow, narrow) + number(ids)
        + low(wide, narrow, narrow) + number(ids) + low(wide, wide)
        + number(ids) + low(narrow, narrow, narrow, wide, packed, packed, packed, packed, narrow)
        + [pltpu.VMEM((DIAG_ROWS, packed[1]), F32)]
        + [pltpu.SemaphoreType.DMA((n,)) for n in (9, 13, 13, splits, splits)],
        compiler_params=pltpu.CompilerParams(
            collective_id=0, has_side_effects=True, vmem_limit_bytes=40 * 2**20
        ),
        cost_estimate=pl.CostEstimate(flops=2**30, bytes_accessed=2**23, transcendentals=2**20),
    )(
        fwd_q[0], fwd_k[0], fwd_v[0], fwd_segments, held_q[0], held_k[0], held_v[0], back_segments, up_grad[0]
    )
    return tuple(result[None] for result in results)


def solution(mesh):
    heads = P("section", None, "tp")
    tokens = P("section", None)
    return jax.shard_map(
        shards,
        mesh=mesh,
        in_specs=(heads, heads, heads, tokens, heads, heads, heads, tokens, heads),
        out_specs=(P("section", "tp", None),) + (heads,) * 6,
        check_vma=False,
    )
```

```python
import functools

import jax
import jax.numpy as jnp
from jax import lax
from jax.experimental import pallas as pl
from jax.experimental.pallas import tpu as pltpu
from jax.sharding import PartitionSpec as P

HQ = 64
KV = 8
HD = 128
GROUP = HQ // KV
SCALE = HD**-0.5
LOW = jnp.bfloat16
F32 = jnp.float32
DIAG_ROWS = 16
MESH = pl.DeviceIdType.MESH


def dot_nt(a, b):
    return lax.dot_general(a, b, (((1,), (1,)), ((), ())), preferred_element_type=F32)


def dot_tn(a, b):
    return lax.dot_general(a, b, (((0,), (0,)), ((), ())), preferred_element_type=F32)


def dot_nn(a, b):
    return lax.dot_general(a, b, (((1,), (0,)), ((), ())), preferred_element_type=F32)


def iotas(shape):
    return lax.broadcasted_iota(jnp.int32, shape, 0), lax.broadcasted_iota(jnp.int32, shape, 1)


def segment_sides(ids_ref):
    tokens = ids_ref.shape[1]
    across = jnp.broadcast_to(ids_ref[...].astype(F32), (tokens, tokens))
    return across.T, across


def allowed_mask(down, across):
    rows, cols = iotas(down.shape)
    return (down == across) & (cols <= rows)


def probability(q, k, allowed):
    scores = jnp.where(allowed, dot_nt(q, k) * SCALE, -jnp.inf)
    weights = jnp.exp(scores - jnp.max(scores, axis=1, keepdims=True))
    return weights / jnp.sum(weights, axis=1, keepdims=True)


def pack(full):
    half = full.shape[0] // 2
    rows, cols = iotas((half, half))
    turned = full[half:, :].T
    packed = full[:half, :half] + turned[:half] + jnp.where(rows < cols, turned[half:], 0.0)
    diag = jnp.sum(jnp.where(rows == cols, full[half:, half:], 0.0), axis=0, keepdims=True)
    return packed, diag


def unpack_masks(down, across):
    half = down.shape[0] // 2
    rows, cols = iotas((half, half))
    first = (down[:half, :half] == across[:half, :half]) & (cols <= rows)
    cross = down[:half, :half] == across[:half, half:]
    second = (down[half:, half:] == across[half:, half:]) & (rows < cols)
    return first, jnp.concatenate([cross, second], axis=0), rows == cols


def unpack(packed, diag, masks):
    first, turned_mask, eye = masks
    turned = jnp.where(turned_mask, jnp.concatenate([packed, packed], axis=0), 0.0).T
    half = packed.shape[0]
    zero = jnp.zeros((half, half), F32)
    on_diag = jnp.where(eye, jnp.broadcast_to(diag, (half, half)), 0.0)
    top = jnp.concatenate([jnp.where(first, packed, 0.0), zero], axis=1)
    bottom = turned + jnp.concatenate([zero, on_diag], axis=1)
    return jnp.concatenate([top, bottom], axis=0)


def store_packed(g, parts, diag_scratch, pack_ref):
    half = parts[0][0].shape[0]
    values = jnp.concatenate([p for p, _ in parts], axis=1).astype(LOW)
    pack_ref[pl.ds(pl.multiple_of(g * half, half), half), :] = values
    diags = jnp.concatenate([d for _, d in parts], axis=1)
    rows, _ = iotas(diag_scratch.shape)
    diag_scratch[...] = jnp.where(rows == g, jnp.broadcast_to(diags, rows.shape), diag_scratch[...])


def load_packed(g, pack_ref):
    half = pack_ref.shape[1] // GROUP
    values = pack_ref[pl.ds(pl.multiple_of(g * half, half), half), :].astype(F32)
    tail = pack_ref[pl.ds(pack_ref.shape[0] - DIAG_ROWS, DIAG_ROWS), :].astype(F32)
    rows, _ = iotas(tail.shape)
    diags = jnp.sum(jnp.where(rows == g, tail, 0.0), axis=0, keepdims=True)
    return [
        (values[:, h * half : (h + 1) * half], diags[:, h * half : (h + 1) * half]) for h in range(GROUP)
    ]


def head(g, h):
    return pl.ds(pl.multiple_of((g * GROUP + h) * HD, HD), HD)


def own(g):
    return pl.ds(pl.multiple_of(g * HD, HD), HD)


def score_gradient(prob, grad, v):
    dprob = dot_nt(grad, v)
    delta = jnp.sum(prob * dprob, axis=1, keepdims=True)
    return prob * (dprob - delta) * SCALE


def every_group(kv_local, body):
    lax.fori_loop(0, kv_local, lambda g, carry: (body(g), carry)[1], 0)


def tick(
    sections, splits,
    fwd_q, fwd_k, fwd_v, fwd_ids, held_q, held_k, held_v, back_ids, up_grad,
    passed, evicted_q, evicted_k, evicted_v, grad_q, grad_k, grad_v,
    fq, fk, fv, fids, hq, hk, hv, bids, ug,
    out, near, holder_ids, far_ids, keys, third, third_in, arriving, pack_out, pack_in, score_out, score_in, gk, diag,
    load_sem, send_sem, recv_sem, out_send, out_recv, near_send, near_recv,
):
    me, lane = lax.axis_index("section"), lax.axis_index("tp")
    mirror = sections - 1 - me
    right, left = lax.rem(me + 1, sections), lax.rem(me + sections - 1, sections)
    section_short = right == mirror
    holder_short = lax.rem(mirror + 1, sections) == me
    tokens = hq.shape[0]
    kv_local = hk.shape[1] // HD
    rows = tokens // splits
    width = hq.shape[1]

    pairs = [(held_q, hq), (held_k, hk), (held_v, hv), (up_grad, ug), (fwd_q, fq), (fwd_k, fk), (fwd_v, fv),
             (fwd_ids, fids), (back_ids, bids)]
    loads = [pltpu.make_async_copy(src, dst, load_sem.at[n]) for n, (src, dst) in enumerate(pairs)]
    for load in loads:
        load.start()

    barrier = pltpu.get_barrier_semaphore()
    pl.semaphore_signal(barrier, inc=1, device_id=(mirror, lane), device_id_type=MESH)
    for t in range(splits):
        pl.semaphore_signal(barrier, inc=1, device_id=(left, t), device_id_type=MESH)
        pl.semaphore_signal(barrier, inc=1, device_id=(right, t), device_id_type=MESH)
    for t in range(1, splits):
        peer = lax.rem(lane + t, splits)
        pl.semaphore_signal(barrier, inc=1, device_id=(me, peer), device_id_type=MESH)
    pl.semaphore_wait(barrier, 3 * splits)

    def remote(n, src, dst, section):
        return pltpu.make_async_remote_copy(
            src_ref=src, dst_ref=dst, send_sem=send_sem.at[n], recv_sem=recv_sem.at[n],
            device_id=(section, lane), device_id_type=MESH,
        )

    chunk = tokens // 4
    send_ids = remote(0, back_ids, holder_ids, mirror)
    send_keys = remote(1, held_k, keys, mirror)
    send_ek = remote(2, fwd_k, evicted_k, mirror)
    send_ev = remote(3, fwd_v, evicted_v, mirror)
    send_pack = remote(4, pack_out, pack_in, mirror)
    send_third = remote(5, third, third_in, mirror)
    send_score = remote(6, score_out, score_in, mirror)
    send_gk = remote(7, gk, grad_k, mirror)
    send_up = remote(8, up_grad, arriving, left)
    send_eq = [
        remote(9 + c, fwd_q.at[pl.ds(c * chunk, chunk)], evicted_q.at[pl.ds(c * chunk, chunk)], mirror)
        for c in range(4)
    ]
    send_far = remote(13, fwd_ids, far_ids, mirror)
    send_out, send_near = [], []
    for offset in range(splits):
        to = lax.rem(lane + offset, splits)
        send_out.append(
            pltpu.make_async_remote_copy(
                src_ref=out.at[pl.ds(pl.multiple_of(to * rows, rows), rows)],
                dst_ref=passed.at[:, pl.ds(pl.multiple_of(lane * width, width), width)],
                send_sem=out_send.at[offset], recv_sem=out_recv.at[offset],
                device_id=(right, to), device_id_type=MESH,
            )
        )
        near_rows = near.at[pl.ds(pl.multiple_of(to * rows, rows), rows)]
        columns = passed.at[:, pl.ds(pl.multiple_of(lane * width, width), width)]
        if offset == 0:
            send_near.append(pltpu.make_async_copy(near_rows, columns, near_send.at[0]))
        else:
            send_near.append(
                pltpu.make_async_remote_copy(
                    src_ref=near_rows, dst_ref=columns,
                    send_sem=near_send.at[offset], recv_sem=near_recv.at[offset],
                    device_id=(me, to), device_id_type=MESH,
                )
            )

    send_ids.start()
    send_far.start()
    send_keys.start()
    send_ek.start()

    @pl.when(jnp.logical_not(holder_short))
    def _():
        send_up.start()

    diag[...] = jnp.zeros(diag.shape, F32)

    def close_pack(ref):
        ref[pl.ds(ref.shape[0] - DIAG_ROWS, DIAG_ROWS), :] = diag[...].astype(LOW)

    for load in loads[:4]:
        load.wait()
    send_ids.wait_recv()

    @pl.when(jnp.logical_not(holder_short))
    def _():
        allowed = allowed_mask(*segment_sides(holder_ids))

        def group(g):
            k = hk[:, own(g)]
            parts = [pack(probability(hq[:, head(g, h)], k, allowed)) for h in range(GROUP)]
            store_packed(g, parts, diag, pack_out)

        every_group(kv_local, group)
        third[...] = hv[...]

    @pl.when(holder_short)
    def _():
        allowed = allowed_mask(*segment_sides(holder_ids))

        def group(g):
            k, v = hk[:, own(g)], hv[:, own(g)]
            total = jnp.zeros((tokens, HD), F32)
            parts = []
            for h in range(GROUP):
                prob = probability(hq[:, head(g, h)], k, allowed)
                grad = ug[:, head(g, h)]
                total = total + dot_tn(prob.astype(LOW), grad)
                parts.append(pack(score_gradient(prob, grad, v)))
            store_packed(g, parts, diag, pack_out)
            third[:, own(g)] = total.astype(LOW)

        every_group(kv_local, group)

    close_pack(pack_out)
    send_pack.start()
    send_third.start()
    send_ev.start()
    send_eq[0].start()
    send_eq[1].start()

    @pl.when(section_short)
    def _():
        send_eq[2].start()
        send_eq[3].start()

    for load in loads[4:]:
        load.wait()

    def run_forward(ids_ref, out_ref):
        allowed = allowed_mask(*segment_sides(ids_ref))

        def group(g):
            k, v = fk[:, own(g)], fv[:, own(g)]
            for h in range(GROUP):
                prob = probability(fq[:, head(g, h)], k, allowed)
                out_ref[:, head(g, h)] = dot_nn(prob.astype(LOW), v).astype(LOW)

        every_group(kv_local, group)

    @pl.when(jnp.logical_not(section_short))
    def _():
        run_forward(fids, out)
        for send in send_out:
            send.start()

    send_keys.wait_recv()
    send_pack.wait_recv()
    send_third.wait_recv()
    masks = unpack_masks(*segment_sides(bids))

    @pl.when(jnp.logical_not(section_short))
    def _():
        send_up.wait_recv()

        def group(g):
            k, v = keys[:, own(g)], third_in[:, own(g)]
            total = jnp.zeros((tokens, HD), F32)
            parts = []
            for h, (packed, on_diag) in enumerate(load_packed(g, pack_in)):
                prob = unpack(packed, on_diag, masks)
                grad = arriving[:, head(g, h)]
                total = total + dot_tn(prob.astype(LOW), grad)
                dscore = score_gradient(prob, grad, v)
                grad_q[:, head(g, h)] = dot_nn(dscore.astype(LOW), k).astype(LOW)
                parts.append(pack(dscore))
            store_packed(g, parts, diag, score_out)
            grad_v[:, own(g)] = total.astype(LOW)

        every_group(kv_local, group)
        close_pack(score_out)
        send_score.start()
        send_eq[2].start()

    @pl.when(section_short)
    def _():
        def group(g):
            k = keys[:, own(g)]
            for h, (packed, on_diag) in enumerate(load_packed(g, pack_in)):
                dscore = unpack(packed, on_diag, masks)
                grad_q[:, head(g, h)] = dot_nn(dscore.astype(LOW), k).astype(LOW)

        every_group(kv_local, group)
        grad_v[...] = third_in[...]

    def key_gradient(ref):
        holder_masks = unpack_masks(*segment_sides(holder_ids))

        def group(g):
            total = jnp.zeros((tokens, HD), F32)
            for h, (packed, on_diag) in enumerate(load_packed(g, ref)):
                dscore = unpack(packed, on_diag, holder_masks).astype(LOW)
                total = total + dot_tn(dscore, hq[:, head(g, h)])
            gk[:, own(g)] = total.astype(LOW)

        every_group(kv_local, group)

    @pl.when(holder_short)
    def _():
        key_gradient(pack_out)

    @pl.when(jnp.logical_not(holder_short))
    def _():
        send_score.wait_recv()
        key_gradient(score_in)

    send_gk.start()

    @pl.when(jnp.logical_not(section_short))
    def _():
        send_eq[3].start()

    for send in [send_ek, send_ev, send_far] + send_eq:
        send.wait_recv()

    @pl.when(holder_short)
    def _():
        again = [
            pltpu.make_async_copy(src, dst, load_sem.at[4 + n])
            for n, (src, dst) in enumerate([(evicted_q, fq), (evicted_k, fk), (evicted_v, fv)])
        ]
        for load in again:
            load.start()
        for load in again:
            load.wait()
        run_forward(far_ids, near)
        for send in send_near:
            send.start()
        for send in send_near:
            send.wait()

    @pl.when(jnp.logical_not(holder_short))
    def _():
        for send in send_out:
            send.wait_recv()

    for send in [send_ids, send_far, send_keys, send_ek, send_ev, send_pack, send_third, send_gk] + send_eq:
        send.wait_send()

    @pl.when(jnp.logical_not(holder_short))
    def _():
        send_up.wait_send()

    @pl.when(jnp.logical_not(section_short))
    def _():
        send_score.wait_send()
        for send in send_out:
            send.wait_send()

    send_gk.wait_recv()


def write_all(*refs):
    count = len(refs) // 2
    sems = refs[-1]
    copies = [pltpu.make_async_copy(refs[n], refs[count + n], sems.at[n]) for n in range(count)]
    for copy in copies:
        copy.start()
    for copy in copies:
        copy.wait()


def shards(fwd_q, fwd_k, fwd_v, fwd_segments, held_q, held_k, held_v, back_segments, up_grad):
    sections, splits = lax.axis_size("section"), lax.axis_size("tp")
    tokens, width = held_q.shape[1], held_q.shape[2]
    narrow_width = held_k.shape[2]
    kv_local = narrow_width // HD
    wide, narrow, ids = (tokens, width), (tokens, narrow_width), (1, tokens)
    packed = (kv_local * (tokens // 2) + DIAG_ROWS, GROUP * (tokens // 2))
    passed = (tokens // splits, splits * width)
    anywhere, vmem = pl.BlockSpec(memory_space=pl.ANY), pl.BlockSpec(memory_space=pltpu.VMEM)

    def low(*shapes):
        return [pltpu.VMEM(shape, LOW) for shape in shapes]

    def number(*shapes):
        return [pltpu.VMEM(shape, jnp.int32) for shape in shapes]

    results = pl.pallas_call(
        functools.partial(tick, sections, splits),
        in_specs=[pl.BlockSpec(memory_space=pltpu.HBM)] * 9,
        out_specs=[anywhere] * 4 + [vmem, anywhere, vmem],
        out_shape=[jax.ShapeDtypeStruct(s, LOW) for s in (passed, wide, narrow, narrow, wide, narrow, narrow)],
        scratch_shapes=low(wide, narrow, narrow) + number(ids)
        + low(wide, narrow, narrow) + number(ids) + low(wide, wide, wide)
        + number(ids, ids) + low(narrow, narrow, narrow, wide, packed, packed, packed, packed, narrow)
        + [pltpu.VMEM((DIAG_ROWS, packed[1]), F32)]
        + [pltpu.SemaphoreType.DMA((n,)) for n in (9, 14, 14) + (splits,) * 4],
        compiler_params=pltpu.CompilerParams(
            collective_id=0, has_side_effects=True, vmem_limit_bytes=60 * 2**20
        ),
        cost_estimate=pl.CostEstimate(flops=2**30, bytes_accessed=2**23, transcendentals=2**20),
    )(
        fwd_q[0], fwd_k[0], fwd_v[0], fwd_segments, held_q[0], held_k[0], held_v[0], back_segments, up_grad[0]
    )
    results = pl.pallas_call(
        write_all,
        in_specs=[anywhere] * 7,
        out_specs=[pl.BlockSpec(memory_space=pltpu.HBM)] * 7,
        out_shape=[jax.ShapeDtypeStruct(result.shape, LOW) for result in results],
        scratch_shapes=[pltpu.SemaphoreType.DMA((7,))],
        compiler_params=pltpu.CompilerParams(vmem_limit_bytes=60 * 2**20),
    )(*results)
    return tuple(result[None] for result in results)


def solution(mesh):
    heads = P("section", None, "tp")
    tokens = P("section", None)
    return jax.shard_map(
        shards,
        mesh=mesh,
        in_specs=(heads, heads, heads, tokens, heads, heads, heads, tokens, heads),
        out_specs=(P("section", "tp", None),) + (heads,) * 6,
        check_vma=False,
    )
```

```python
import functools

import jax
import jax.numpy as jnp
from jax import lax
from jax.experimental import pallas as pl
from jax.experimental.pallas import tpu as pltpu
from jax.sharding import PartitionSpec as P

HQ = 64
KV = 8
HD = 128
GROUP = HQ // KV
SCALE = HD**-0.5
LOW = jnp.bfloat16
F32 = jnp.float32
MESH = pl.DeviceIdType.MESH


def dot_nt(a, b):
    return lax.dot_general(a, b, (((1,), (1,)), ((), ())), preferred_element_type=F32)


def dot_tn(a, b):
    return lax.dot_general(a, b, (((0,), (0,)), ((), ())), preferred_element_type=F32)


def dot_nn(a, b):
    return lax.dot_general(a, b, (((1,), (0,)), ((), ())), preferred_element_type=F32)


def iotas(shape):
    return lax.broadcasted_iota(jnp.int32, shape, 0), lax.broadcasted_iota(jnp.int32, shape, 1)


def segment_sides(ids_ref):
    tokens = ids_ref.shape[1]
    across = jnp.broadcast_to(ids_ref[...].astype(F32), (tokens, tokens))
    return across.T, across


def allowed_mask(down, across):
    rows, cols = iotas(down.shape)
    return (down == across) & (cols <= rows)


def probability(q, k, allowed):
    scores = jnp.where(allowed, dot_nt(q, k) * SCALE, -jnp.inf)
    weights = jnp.exp(scores - jnp.max(scores, axis=1, keepdims=True))
    return weights / jnp.sum(weights, axis=1, keepdims=True)


def pack(full):
    half = full.shape[0] // 2
    rows, cols = iotas((half, half))
    turned = full[half:, :].T
    packed = full[:half, :half] + turned[:half] + jnp.where(rows < cols, turned[half:], 0.0)
    diag = jnp.sum(jnp.where(rows == cols, full[half:, half:], 0.0), axis=0, keepdims=True)
    return packed, diag


def unpack_masks(down, across):
    half = down.shape[0] // 2
    rows, cols = iotas((half, half))
    first = (down[:half, :half] == across[:half, :half]) & (cols <= rows)
    cross = down[:half, :half] == across[:half, half:]
    second = (down[half:, half:] == across[half:, half:]) & (rows < cols)
    return first, jnp.concatenate([cross, second], axis=0), rows == cols


def unpack(packed, diag, masks):
    first, turned_mask, eye = masks
    turned = jnp.where(turned_mask, jnp.concatenate([packed, packed], axis=0), 0.0).T
    half = packed.shape[0]
    zero = jnp.zeros((half, half), F32)
    on_diag = jnp.where(eye, jnp.broadcast_to(diag, (half, half)), 0.0)
    top = jnp.concatenate([jnp.where(first, packed, 0.0), zero], axis=1)
    bottom = turned + jnp.concatenate([zero, on_diag], axis=1)
    return jnp.concatenate([top, bottom], axis=0)


def diag_rows(kv_local, tokens):
    rows = kv_local * GROUP * (tokens // 2) // HD
    return -(-rows // 16) * 16


def store_packed(g, parts, diag_scratch, pack_ref):
    half = parts[0][0].shape[0]
    values = jnp.concatenate([p for p, _ in parts], axis=1).astype(LOW)
    pack_ref[pl.ds(pl.multiple_of(g * half, half), half), :] = values
    diags = jnp.concatenate([d for _, d in parts], axis=1)
    rows, _ = iotas(diag_scratch.shape)
    merged = diag_scratch[...]
    lines = diags.shape[1] // HD
    for c in range(lines):
        line = jnp.broadcast_to(diags[:, c * HD : (c + 1) * HD], rows.shape)
        merged = jnp.where(rows == g * lines + c, line, merged)
    diag_scratch[...] = merged


def load_packed(g, pack_ref, diag_ref):
    half = pack_ref.shape[1] // GROUP
    values = pack_ref[pl.ds(pl.multiple_of(g * half, half), half), :].astype(F32)
    tail = diag_ref[...].astype(F32)
    rows, _ = iotas(tail.shape)
    lines = pack_ref.shape[1] // HD
    found = [jnp.sum(jnp.where(rows == g * lines + c, tail, 0.0), axis=0, keepdims=True) for c in range(lines)]
    diags = jnp.concatenate(found, axis=1)
    return [
        (values[:, h * half : (h + 1) * half], diags[:, h * half : (h + 1) * half]) for h in range(GROUP)
    ]


def head(g, h):
    return pl.ds(pl.multiple_of((g * GROUP + h) * HD, HD), HD)


def own(g):
    return pl.ds(pl.multiple_of(g * HD, HD), HD)


def score_gradient(prob, grad, v):
    dprob = dot_nt(grad, v)
    delta = jnp.sum(prob * dprob, axis=1, keepdims=True)
    return prob * (dprob - delta) * SCALE


def every_group(kv_local, body):
    lax.fori_loop(0, kv_local, lambda g, carry: (body(g), carry)[1], 0)


def tick(
    sections, splits,
    fwd_q, fwd_k, fwd_v, fwd_ids, held_q, held_k, held_v, back_ids, up_grad,
    passed, evicted_q, evicted_k, evicted_v, grad_q, grad_k, grad_v,
    fq, fk, fv, fids, hq, hk, hv, bids, ug,
    out, near, holder_ids, far_ids, keys, third, third_in, arriving, pack_out, pack_in, score_out, score_in, pack_dout, pack_din, score_dout, score_din, gk, diag,
    load_sem, send_sem, recv_sem, out_send, out_recv, near_send, near_recv,
):
    me, lane = lax.axis_index("section"), lax.axis_index("tp")
    mirror = sections - 1 - me
    right, left = lax.rem(me + 1, sections), lax.rem(me + sections - 1, sections)
    section_short = right == mirror
    holder_short = lax.rem(mirror + 1, sections) == me
    tokens = hq.shape[0]
    kv_local = hk.shape[1] // HD
    rows = tokens // splits
    width = hq.shape[1]

    pairs = [(held_q, hq), (held_k, hk), (held_v, hv), (up_grad, ug), (fwd_q, fq), (fwd_k, fk), (fwd_v, fv),
             (fwd_ids, fids), (back_ids, bids)]
    loads = [pltpu.make_async_copy(src, dst, load_sem.at[n]) for n, (src, dst) in enumerate(pairs)]
    for load in loads:
        load.start()

    barrier = pltpu.get_barrier_semaphore()
    pl.semaphore_signal(barrier, inc=1, device_id=(mirror, lane), device_id_type=MESH)
    for t in range(splits):
        pl.semaphore_signal(barrier, inc=1, device_id=(left, t), device_id_type=MESH)
        pl.semaphore_signal(barrier, inc=1, device_id=(right, t), device_id_type=MESH)
    for t in range(1, splits):
        peer = lax.rem(lane + t, splits)
        pl.semaphore_signal(barrier, inc=1, device_id=(me, peer), device_id_type=MESH)
    pl.semaphore_wait(barrier, 3 * splits)

    def remote(n, src, dst, section):
        return pltpu.make_async_remote_copy(
            src_ref=src, dst_ref=dst, send_sem=send_sem.at[n], recv_sem=recv_sem.at[n],
            device_id=(section, lane), device_id_type=MESH,
        )


    def block(g, base=0):
        return pl.ds(pl.multiple_of(base + g * GROUP * HD, GROUP * HD), GROUP * HD)

    send_ids = remote(0, back_ids, holder_ids, mirror)
    send_keys = remote(1, held_k, keys, mirror)
    send_ek = remote(2, fwd_k, evicted_k, mirror)
    send_ev = remote(3, fwd_v, evicted_v, mirror)
    send_pack = remote(4, pack_out, pack_in, mirror)
    send_third = remote(5, third, third_in, mirror)
    send_score = remote(6, score_out, score_in, mirror)
    send_gk = remote(7, gk, grad_k, mirror)
    send_up = remote(8, up_grad, arriving, left)
    send_pack_diag = remote(9, pack_dout, pack_din, mirror)
    send_score_diag = remote(10, score_dout, score_din, mirror)
    send_eq = [remote(12 + g, fwd_q.at[:, block(g)], evicted_q.at[:, block(g)], mirror) for g in range(kv_local)]
    early, middle = (kv_local + 1) // 2, (3 * kv_local + 3) // 4
    send_far = remote(11, fwd_ids, far_ids, mirror)
    send_out = []
    for offset in range(splits):
        to = lax.rem(lane + offset, splits)
        send_out.append(
            pltpu.make_async_remote_copy(
                src_ref=out.at[pl.ds(pl.multiple_of(to * rows, rows), rows)],
                dst_ref=passed.at[:, pl.ds(pl.multiple_of(lane * width, width), width)],
                send_sem=out_send.at[offset], recv_sem=out_recv.at[offset],
                device_id=(right, to), device_id_type=MESH,
            )
        )

    def near_copies(g):
        copies = []
        for offset in range(splits):
            to = lax.rem(lane + offset, splits)
            src = near.at[pl.ds(pl.multiple_of(to * rows, rows), rows), block(g)]
            dst = passed.at[:, block(g, lane * width)]
            n = offset * kv_local + g
            if offset == 0:
                copies.append(pltpu.make_async_copy(src, dst, near_send.at[n]))
            else:
                copies.append(
                    pltpu.make_async_remote_copy(
                        src_ref=src, dst_ref=dst, send_sem=near_send.at[n], recv_sem=near_recv.at[n],
                        device_id=(me, to), device_id_type=MESH,
                    )
                )
        return copies

    send_ids.start()
    send_far.start()
    send_keys.start()
    send_ek.start()
    send_ev.start()

    @pl.when(jnp.logical_not(holder_short))
    def _():
        send_up.start()

    diag[...] = jnp.zeros(diag.shape, F32)

    for load in loads[:4]:
        load.wait()
    send_ids.wait_recv()

    @pl.when(jnp.logical_not(holder_short))
    def _():
        allowed = allowed_mask(*segment_sides(holder_ids))

        def group(g):
            k = hk[:, own(g)]
            parts = [pack(probability(hq[:, head(g, h)], k, allowed)) for h in range(GROUP)]
            store_packed(g, parts, diag, pack_out)

        every_group(kv_local, group)
        third[...] = hv[...]

    @pl.when(holder_short)
    def _():
        allowed = allowed_mask(*segment_sides(holder_ids))

        def group(g):
            k, v = hk[:, own(g)], hv[:, own(g)]
            total = jnp.zeros((tokens, HD), F32)
            parts = []
            for h in range(GROUP):
                prob = probability(hq[:, head(g, h)], k, allowed)
                grad = ug[:, head(g, h)]
                total = total + dot_tn(prob.astype(LOW), grad)
                parts.append(pack(score_gradient(prob, grad, v)))
            store_packed(g, parts, diag, pack_out)
            third[:, own(g)] = total.astype(LOW)

        every_group(kv_local, group)

    pack_dout[...] = diag[...].astype(LOW)
    send_pack.start()
    send_pack_diag.start()
    send_third.start()
    for send in send_eq[:early]:
        send.start()

    @pl.when(section_short)
    def _():
        for send in send_eq[early:]:
            send.start()

    for load in loads[4:]:
        load.wait()

    def forward_group(allowed, out_ref, g):
        k, v = fk[:, own(g)], fv[:, own(g)]
        for h in range(GROUP):
            prob = probability(fq[:, head(g, h)], k, allowed)
            out_ref[:, head(g, h)] = dot_nn(prob.astype(LOW), v).astype(LOW)

    @pl.when(jnp.logical_not(section_short))
    def _():
        every_group(kv_local, functools.partial(forward_group, allowed_mask(*segment_sides(fids)), out))
        for send in send_out:
            send.start()

    send_keys.wait_recv()
    send_pack.wait_recv()
    send_pack_diag.wait_recv()
    send_third.wait_recv()
    masks = unpack_masks(*segment_sides(bids))

    @pl.when(jnp.logical_not(section_short))
    def _():
        send_up.wait_recv()

        def group(g):
            k, v = keys[:, own(g)], third_in[:, own(g)]
            total = jnp.zeros((tokens, HD), F32)
            parts = []
            for h, (packed, on_diag) in enumerate(load_packed(g, pack_in, pack_din)):
                prob = unpack(packed, on_diag, masks)
                grad = arriving[:, head(g, h)]
                total = total + dot_tn(prob.astype(LOW), grad)
                dscore = score_gradient(prob, grad, v)
                grad_q[:, head(g, h)] = dot_nn(dscore.astype(LOW), k).astype(LOW)
                parts.append(pack(dscore))
            store_packed(g, parts, diag, score_out)
            grad_v[:, own(g)] = total.astype(LOW)

        every_group(kv_local, group)
        score_dout[...] = diag[...].astype(LOW)
        send_score.start()
        send_score_diag.start()
        for send in send_eq[early:middle]:
            send.start()

    @pl.when(section_short)
    def _():
        def group(g):
            k = keys[:, own(g)]
            for h, (packed, on_diag) in enumerate(load_packed(g, pack_in, pack_din)):
                dscore = unpack(packed, on_diag, masks)
                grad_q[:, head(g, h)] = dot_nn(dscore.astype(LOW), k).astype(LOW)

        every_group(kv_local, group)
        grad_v[...] = third_in[...]

    def key_gradient(ref, diag_ref):
        holder_masks = unpack_masks(*segment_sides(holder_ids))

        def group(g):
            total = jnp.zeros((tokens, HD), F32)
            for h, (packed, on_diag) in enumerate(load_packed(g, ref, diag_ref)):
                dscore = unpack(packed, on_diag, holder_masks).astype(LOW)
                total = total + dot_tn(dscore, hq[:, head(g, h)])
            gk[:, own(g)] = total.astype(LOW)

        every_group(kv_local, group)

    @pl.when(holder_short)
    def _():
        key_gradient(pack_out, pack_dout)

    @pl.when(jnp.logical_not(holder_short))
    def _():
        send_score.wait_recv()
        send_score_diag.wait_recv()
        key_gradient(score_in, score_din)

    send_gk.start()

    @pl.when(jnp.logical_not(section_short))
    def _():
        for send in send_eq[middle:]:
            send.start()

    for send in [send_ek, send_ev, send_far]:
        send.wait_recv()

    @pl.when(holder_short)
    def _():
        again = [
            pltpu.make_async_copy(src, dst, load_sem.at[4 + n])
            for n, (src, dst) in enumerate([(evicted_k, fk), (evicted_v, fv)])
        ]
        for load in again:
            load.start()
        for load in again:
            load.wait()
        allowed = allowed_mask(*segment_sides(far_ids))
        for g in range(kv_local):
            send_eq[g].wait_recv()
            load = pltpu.make_async_copy(evicted_q.at[:, block(g)], fq.at[:, block(g)], load_sem.at[6])
            load.start()
            load.wait()
            forward_group(allowed, near, g)
            for copy in near_copies(g):
                copy.start()
        for g in range(kv_local):
            for copy in near_copies(g):
                copy.wait()

    @pl.when(jnp.logical_not(holder_short))
    def _():
        for send in send_eq:
            send.wait_recv()

    @pl.when(jnp.logical_not(holder_short))
    def _():
        for send in send_out:
            send.wait_recv()

    for send in [send_ids, send_far, send_keys, send_ek, send_ev, send_pack, send_pack_diag, send_third, send_gk] + send_eq:
        send.wait_send()

    @pl.when(jnp.logical_not(holder_short))
    def _():
        send_up.wait_send()

    @pl.when(jnp.logical_not(section_short))
    def _():
        send_score.wait_send()
        send_score_diag.wait_send()
        for send in send_out:
            send.wait_send()

    send_gk.wait_recv()


def write_all(*refs):
    count = (len(refs) - 2) // 3
    here, there, rooms = refs[:count], refs[count : 2 * count], refs[2 * count : 3 * count]
    in_sem, out_sem = refs[3 * count :]
    reads = [pltpu.make_async_copy(here[n], rooms[n], in_sem.at[n]) for n in range(count)]
    writes = [pltpu.make_async_copy(rooms[n], there[n], out_sem.at[n]) for n in range(count)]
    for read in reads:
        read.start()
    for read, write in zip(reads, writes):
        read.wait()
        write.start()
    for write in writes:
        write.wait()


def shards(fwd_q, fwd_k, fwd_v, fwd_segments, held_q, held_k, held_v, back_segments, up_grad):
    sections, splits = lax.axis_size("section"), lax.axis_size("tp")
    tokens, width = held_q.shape[1], held_q.shape[2]
    narrow_width = held_k.shape[2]
    kv_local = narrow_width // HD
    wide, narrow, ids = (tokens, width), (tokens, narrow_width), (1, tokens)
    packed = (kv_local * (tokens // 2), GROUP * (tokens // 2))
    diags = (diag_rows(kv_local, tokens), HD)
    passed = (tokens // splits, splits * width)
    anywhere, vmem = pl.BlockSpec(memory_space=pl.ANY), pl.BlockSpec(memory_space=pltpu.VMEM)

    def low(*shapes):
        return [pltpu.VMEM(shape, LOW) for shape in shapes]

    def number(*shapes):
        return [pltpu.VMEM(shape, jnp.int32) for shape in shapes]

    results = pl.pallas_call(
        functools.partial(tick, sections, splits),
        in_specs=[pl.BlockSpec(memory_space=pltpu.HBM)] * 9,
        out_specs=[anywhere] * 4 + [vmem, anywhere, vmem],
        out_shape=[jax.ShapeDtypeStruct(s, LOW) for s in (passed, wide, narrow, narrow, wide, narrow, narrow)],
        scratch_shapes=low(wide, narrow, narrow) + number(ids)
        + low(wide, narrow, narrow) + number(ids) + low(wide, wide, wide)
        + number(ids, ids) + low(narrow, narrow, narrow, wide, packed, packed, packed, packed, diags, diags, diags, diags, narrow)
        + [pltpu.VMEM(diags, F32)]
        + [pltpu.SemaphoreType.DMA((n,)) for n in (9, 12 + kv_local, 12 + kv_local, splits, splits, splits * kv_local, splits * kv_local)],
        compiler_params=pltpu.CompilerParams(
            collective_id=0, has_side_effects=True, vmem_limit_bytes=60 * 2**20
        ),
        cost_estimate=pl.CostEstimate(flops=2**30, bytes_accessed=2**23, transcendentals=2**20),
    )(
        fwd_q[0], fwd_k[0], fwd_v[0], fwd_segments, held_q[0], held_k[0], held_v[0], back_segments, up_grad[0]
    )
    results = pl.pallas_call(
        write_all,
        in_specs=[anywhere] * 7,
        out_specs=[pl.BlockSpec(memory_space=pltpu.HBM)] * 7,
        out_shape=[jax.ShapeDtypeStruct(result.shape, LOW) for result in results],
        scratch_shapes=[pltpu.VMEM(result.shape, LOW) for result in results] + [pltpu.SemaphoreType.DMA((7,))] * 2,
        compiler_params=pltpu.CompilerParams(vmem_limit_bytes=60 * 2**20),
    )(*results)
    return tuple(result[None] for result in results)


def solution(mesh):
    heads = P("section", None, "tp")
    tokens = P("section", None)
    return jax.shard_map(
        shards,
        mesh=mesh,
        in_specs=(heads, heads, heads, tokens, heads, heads, heads, tokens, heads),
        out_specs=(P("section", "tp", None),) + (heads,) * 6,
        check_vma=False,
    )
```

```python
import functools

import jax
import jax.numpy as jnp
from jax import lax
from jax.experimental import pallas as pl
from jax.experimental.pallas import tpu as pltpu
from jax.sharding import PartitionSpec as P

HQ = 64
KV = 8
HD = 128
GROUP = HQ // KV
SCALE = HD**-0.5
LOW = jnp.bfloat16
F32 = jnp.float32
MESH = pl.DeviceIdType.MESH


def dot_nt(a, b):
    return lax.dot_general(a, b, (((1,), (1,)), ((), ())), preferred_element_type=F32)


def dot_tn(a, b):
    return lax.dot_general(a, b, (((0,), (0,)), ((), ())), preferred_element_type=F32)


def dot_nn(a, b):
    return lax.dot_general(a, b, (((1,), (0,)), ((), ())), preferred_element_type=F32)


def iotas(shape):
    return lax.broadcasted_iota(jnp.int32, shape, 0), lax.broadcasted_iota(jnp.int32, shape, 1)


def segment_sides(ids_ref):
    tokens = ids_ref.shape[1]
    across = jnp.broadcast_to(ids_ref[...].astype(F32), (tokens, tokens))
    return across.T, across


def allowed_mask(down, across):
    rows, cols = iotas(down.shape)
    return (down == across) & (cols <= rows)


def probability(q, k, allowed):
    scores = jnp.where(allowed, dot_nt(q, k) * SCALE, -jnp.inf)
    weights = jnp.exp(scores - jnp.max(scores, axis=1, keepdims=True))
    return weights / jnp.sum(weights, axis=1, keepdims=True)


def pack(full):
    half = full.shape[0] // 2
    rows, cols = iotas((half, half))
    turned = full[half:, :].T
    packed = full[:half, :half] + turned[:half] + jnp.where(rows < cols, turned[half:], 0.0)
    diag = jnp.sum(jnp.where(rows == cols, full[half:, half:], 0.0), axis=0, keepdims=True)
    return packed, diag


def unpack_masks(down, across):
    half = down.shape[0] // 2
    rows, cols = iotas((half, half))
    first = (down[:half, :half] == across[:half, :half]) & (cols <= rows)
    cross = down[:half, :half] == across[:half, half:]
    second = (down[half:, half:] == across[half:, half:]) & (rows < cols)
    return first, jnp.concatenate([cross, second], axis=0), rows == cols


def unpack(packed, diag, masks):
    first, turned_mask, eye = masks
    turned = jnp.where(turned_mask, jnp.concatenate([packed, packed], axis=0), 0.0).T
    half = packed.shape[0]
    zero = jnp.zeros((half, half), F32)
    on_diag = jnp.where(eye, jnp.broadcast_to(diag, (half, half)), 0.0)
    top = jnp.concatenate([jnp.where(first, packed, 0.0), zero], axis=1)
    bottom = turned + jnp.concatenate([zero, on_diag], axis=1)
    return jnp.concatenate([top, bottom], axis=0)


def diag_rows(kv_local, tokens):
    rows = kv_local * GROUP * (tokens // 2) // HD
    return -(-rows // 16) * 16


def store_packed(g, parts, diag_scratch, pack_ref):
    half = parts[0][0].shape[0]
    values = jnp.concatenate([p for p, _ in parts], axis=1).astype(LOW)
    pack_ref[pl.ds(pl.multiple_of(g * half, half), half), :] = values
    diags = jnp.concatenate([d for _, d in parts], axis=1)
    rows, _ = iotas(diag_scratch.shape)
    merged = diag_scratch[...]
    lines = diags.shape[1] // HD
    for c in range(lines):
        line = jnp.broadcast_to(diags[:, c * HD : (c + 1) * HD], rows.shape)
        merged = jnp.where(rows == g * lines + c, line, merged)
    diag_scratch[...] = merged


def load_packed(g, pack_ref, diag_ref):
    half = pack_ref.shape[1] // GROUP
    values = pack_ref[pl.ds(pl.multiple_of(g * half, half), half), :].astype(F32)
    tail = diag_ref[...].astype(F32)
    rows, _ = iotas(tail.shape)
    lines = pack_ref.shape[1] // HD
    found = [jnp.sum(jnp.where(rows == g * lines + c, tail, 0.0), axis=0, keepdims=True) for c in range(lines)]
    diags = jnp.concatenate(found, axis=1)
    return [
        (values[:, h * half : (h + 1) * half], diags[:, h * half : (h + 1) * half]) for h in range(GROUP)
    ]


def head(g, h):
    return pl.ds(pl.multiple_of((g * GROUP + h) * HD, HD), HD)


def own(g):
    return pl.ds(pl.multiple_of(g * HD, HD), HD)


def score_gradient(prob, grad, v):
    dprob = dot_nt(grad, v)
    delta = jnp.sum(prob * dprob, axis=1, keepdims=True)
    return prob * (dprob - delta) * SCALE


def every_group(kv_local, body):
    lax.fori_loop(0, kv_local, lambda g, carry: (body(g), carry)[1], 0)


def tick(
    sections, splits,
    fwd_q, fwd_k, fwd_v, fwd_ids, held_q, held_k, held_v, back_ids, up_grad,
    passed, evicted_q, evicted_k, evicted_v, grad_q, grad_k, grad_v,
    fq, fk, fv, fids, hq, hk, hv, bids, ug,
    out, near, holder_ids, far_ids, keys, third, third_in, arriving, pack_out, pack_in, score_out, score_in, pack_dout, pack_din, score_dout, score_din, gk, diag,
    load_sem, send_sem, recv_sem, out_send, out_recv, near_send, near_recv,
):
    me, lane = lax.axis_index("section"), lax.axis_index("tp")
    mirror = sections - 1 - me
    right, left = lax.rem(me + 1, sections), lax.rem(me + sections - 1, sections)
    section_short = right == mirror
    holder_short = lax.rem(mirror + 1, sections) == me
    tokens = hq.shape[0]
    kv_local = hk.shape[1] // HD
    rows = tokens // splits
    width = hq.shape[1]

    pairs = [(held_q, hq), (held_k, hk), (held_v, hv), (up_grad, ug), (fwd_q, fq), (fwd_k, fk), (fwd_v, fv),
             (fwd_ids, fids), (back_ids, bids)]
    loads = [pltpu.make_async_copy(src, dst, load_sem.at[n]) for n, (src, dst) in enumerate(pairs)]
    for load in loads:
        load.start()

    barrier = pltpu.get_barrier_semaphore()
    pl.semaphore_signal(barrier, inc=1, device_id=(mirror, lane), device_id_type=MESH)
    for t in range(splits):
        pl.semaphore_signal(barrier, inc=1, device_id=(left, t), device_id_type=MESH)
        pl.semaphore_signal(barrier, inc=1, device_id=(right, t), device_id_type=MESH)
    for t in range(1, splits):
        peer = lax.rem(lane + t, splits)
        pl.semaphore_signal(barrier, inc=1, device_id=(me, peer), device_id_type=MESH)
    pl.semaphore_wait(barrier, 3 * splits)

    def remote(n, src, dst, section):
        return pltpu.make_async_remote_copy(
            src_ref=src, dst_ref=dst, send_sem=send_sem.at[n], recv_sem=recv_sem.at[n],
            device_id=(section, lane), device_id_type=MESH,
        )


    def block(g, base=0):
        return pl.ds(pl.multiple_of(base + g * GROUP * HD, GROUP * HD), GROUP * HD)

    send_ids = remote(0, back_ids, holder_ids, mirror)
    send_keys = remote(1, held_k, keys, mirror)
    send_ek = remote(2, fwd_k, evicted_k, mirror)
    send_ev = remote(3, fwd_v, evicted_v, mirror)
    send_pack = remote(4, pack_out, pack_in, mirror)
    send_third = remote(5, third, third_in, mirror)
    send_score = remote(6, score_out, score_in, mirror)
    send_gk = remote(7, gk, grad_k, mirror)
    send_up = remote(8, up_grad, arriving, left)
    send_pack_diag = remote(9, pack_dout, pack_din, mirror)
    send_score_diag = remote(10, score_dout, score_din, mirror)
    send_eq = [remote(12 + g, fwd_q.at[:, block(g)], evicted_q.at[:, block(g)], mirror) for g in range(kv_local)]
    early = (kv_local + 1) // 2
    send_far = remote(11, fwd_ids, far_ids, mirror)
    send_out = []
    for offset in range(splits):
        to = lax.rem(lane + offset, splits)
        send_out.append(
            pltpu.make_async_remote_copy(
                src_ref=out.at[pl.ds(pl.multiple_of(to * rows, rows), rows)],
                dst_ref=passed.at[:, pl.ds(pl.multiple_of(lane * width, width), width)],
                send_sem=out_send.at[offset], recv_sem=out_recv.at[offset],
                device_id=(right, to), device_id_type=MESH,
            )
        )

    def near_copies(g):
        copies = []
        for offset in range(splits):
            to = lax.rem(lane + offset, splits)
            src = near.at[pl.ds(pl.multiple_of(to * rows, rows), rows), block(g)]
            dst = passed.at[:, block(g, lane * width)]
            n = offset * kv_local + g
            if offset == 0:
                copies.append(pltpu.make_async_copy(src, dst, near_send.at[n]))
            else:
                copies.append(
                    pltpu.make_async_remote_copy(
                        src_ref=src, dst_ref=dst, send_sem=near_send.at[n], recv_sem=near_recv.at[n],
                        device_id=(me, to), device_id_type=MESH,
                    )
                )
        return copies

    send_ids.start()
    send_far.start()
    send_keys.start()
    send_ek.start()
    send_ev.start()

    @pl.when(jnp.logical_not(holder_short))
    def _():
        send_up.start()

    diag[...] = jnp.zeros(diag.shape, F32)

    for load in loads[:4]:
        load.wait()
    send_ids.wait_recv()

    @pl.when(jnp.logical_not(holder_short))
    def _():
        allowed = allowed_mask(*segment_sides(holder_ids))

        def group(g):
            k = hk[:, own(g)]
            parts = [pack(probability(hq[:, head(g, h)], k, allowed)) for h in range(GROUP)]
            store_packed(g, parts, diag, pack_out)

        every_group(kv_local, group)
        third[...] = hv[...]

    @pl.when(holder_short)
    def _():
        allowed = allowed_mask(*segment_sides(holder_ids))

        def group(g):
            k, v = hk[:, own(g)], hv[:, own(g)]
            total = jnp.zeros((tokens, HD), F32)
            parts = []
            for h in range(GROUP):
                prob = probability(hq[:, head(g, h)], k, allowed)
                grad = ug[:, head(g, h)]
                total = total + dot_tn(prob.astype(LOW), grad)
                parts.append(pack(score_gradient(prob, grad, v)))
            store_packed(g, parts, diag, pack_out)
            third[:, own(g)] = total.astype(LOW)

        every_group(kv_local, group)

    pack_dout[...] = diag[...].astype(LOW)
    send_pack.start()
    send_pack_diag.start()
    send_third.start()
    for send in send_eq[:early]:
        send.start()

    @pl.when(jnp.logical_or(section_short, holder_short))
    def _():
        for send in send_eq[early:]:
            send.start()

    def key_gradient(ref, diag_ref):
        holder_masks = unpack_masks(*segment_sides(holder_ids))

        def group(g):
            total = jnp.zeros((tokens, HD), F32)
            for h, (packed, on_diag) in enumerate(load_packed(g, ref, diag_ref)):
                dscore = unpack(packed, on_diag, holder_masks).astype(LOW)
                total = total + dot_tn(dscore, hq[:, head(g, h)])
            gk[:, own(g)] = total.astype(LOW)

        every_group(kv_local, group)

    @pl.when(holder_short)
    def _():
        key_gradient(pack_out, pack_dout)
        send_gk.start()

    for load in loads[4:]:
        load.wait()

    def forward_group(allowed, out_ref, g):
        k, v = fk[:, own(g)], fv[:, own(g)]
        for h in range(GROUP):
            prob = probability(fq[:, head(g, h)], k, allowed)
            out_ref[:, head(g, h)] = dot_nn(prob.astype(LOW), v).astype(LOW)

    @pl.when(jnp.logical_not(section_short))
    def _():
        every_group(kv_local, functools.partial(forward_group, allowed_mask(*segment_sides(fids)), out))
        for send in send_out:
            send.start()

    send_keys.wait_recv()
    send_pack.wait_recv()
    send_pack_diag.wait_recv()
    send_third.wait_recv()
    masks = unpack_masks(*segment_sides(bids))

    @pl.when(jnp.logical_not(section_short))
    def _():
        send_up.wait_recv()

        def group(g):
            k, v = keys[:, own(g)], third_in[:, own(g)]
            total = jnp.zeros((tokens, HD), F32)
            parts = []
            for h, (packed, on_diag) in enumerate(load_packed(g, pack_in, pack_din)):
                prob = unpack(packed, on_diag, masks)
                grad = arriving[:, head(g, h)]
                total = total + dot_tn(prob.astype(LOW), grad)
                dscore = score_gradient(prob, grad, v)
                grad_q[:, head(g, h)] = dot_nn(dscore.astype(LOW), k).astype(LOW)
                parts.append(pack(dscore))
            store_packed(g, parts, diag, score_out)
            grad_v[:, own(g)] = total.astype(LOW)

        every_group(kv_local, group)
        score_dout[...] = diag[...].astype(LOW)
        send_score.start()
        send_score_diag.start()

        @pl.when(jnp.logical_not(holder_short))
        def _():
            for send in send_eq[early:]:
                send.start()


    @pl.when(section_short)
    def _():
        def group(g):
            k = keys[:, own(g)]
            for h, (packed, on_diag) in enumerate(load_packed(g, pack_in, pack_din)):
                dscore = unpack(packed, on_diag, masks)
                grad_q[:, head(g, h)] = dot_nn(dscore.astype(LOW), k).astype(LOW)

        every_group(kv_local, group)
        grad_v[...] = third_in[...]

    @pl.when(jnp.logical_not(holder_short))
    def _():
        send_score.wait_recv()
        send_score_diag.wait_recv()
        key_gradient(score_in, score_din)
        send_gk.start()


    for send in [send_ek, send_ev, send_far]:
        send.wait_recv()

    @pl.when(holder_short)
    def _():
        again = [
            pltpu.make_async_copy(src, dst, load_sem.at[4 + n])
            for n, (src, dst) in enumerate([(evicted_k, fk), (evicted_v, fv)])
        ]
        for load in again:
            load.start()
        for load in again:
            load.wait()
        allowed = allowed_mask(*segment_sides(far_ids))
        for g in range(kv_local):
            send_eq[g].wait_recv()
            load = pltpu.make_async_copy(evicted_q.at[:, block(g)], fq.at[:, block(g)], load_sem.at[6])
            load.start()
            load.wait()
            forward_group(allowed, near, g)
            for copy in near_copies(g):
                copy.start()
        for g in range(kv_local):
            for copy in near_copies(g):
                copy.wait()

    @pl.when(jnp.logical_not(holder_short))
    def _():
        for send in send_eq:
            send.wait_recv()

    @pl.when(jnp.logical_not(holder_short))
    def _():
        for send in send_out:
            send.wait_recv()

    for send in [send_ids, send_far, send_keys, send_ek, send_ev, send_pack, send_pack_diag, send_third, send_gk] + send_eq:
        send.wait_send()

    @pl.when(jnp.logical_not(holder_short))
    def _():
        send_up.wait_send()

    @pl.when(jnp.logical_not(section_short))
    def _():
        send_score.wait_send()
        send_score_diag.wait_send()
        for send in send_out:
            send.wait_send()

    send_gk.wait_recv()


def write_all(*refs):
    count = (len(refs) - 2) // 3
    here, there, rooms = refs[:count], refs[count : 2 * count], refs[2 * count : 3 * count]
    in_sem, out_sem = refs[3 * count :]
    reads = [pltpu.make_async_copy(here[n], rooms[n], in_sem.at[n]) for n in range(count)]
    writes = [pltpu.make_async_copy(rooms[n], there[n], out_sem.at[n]) for n in range(count)]
    for read in reads:
        read.start()
    for read, write in zip(reads, writes):
        read.wait()
        write.start()
    for write in writes:
        write.wait()


def shards(fwd_q, fwd_k, fwd_v, fwd_segments, held_q, held_k, held_v, back_segments, up_grad):
    sections, splits = lax.axis_size("section"), lax.axis_size("tp")
    tokens, width = held_q.shape[1], held_q.shape[2]
    narrow_width = held_k.shape[2]
    kv_local = narrow_width // HD
    wide, narrow, ids = (tokens, width), (tokens, narrow_width), (1, tokens)
    packed = (kv_local * (tokens // 2), GROUP * (tokens // 2))
    diags = (diag_rows(kv_local, tokens), HD)
    passed = (tokens // splits, splits * width)
    anywhere, vmem = pl.BlockSpec(memory_space=pl.ANY), pl.BlockSpec(memory_space=pltpu.VMEM)

    def low(*shapes):
        return [pltpu.VMEM(shape, LOW) for shape in shapes]

    def number(*shapes):
        return [pltpu.VMEM(shape, jnp.int32) for shape in shapes]

    results = pl.pallas_call(
        functools.partial(tick, sections, splits),
        in_specs=[pl.BlockSpec(memory_space=pltpu.HBM)] * 9,
        out_specs=[anywhere] * 4 + [vmem, anywhere, vmem],
        out_shape=[jax.ShapeDtypeStruct(s, LOW) for s in (passed, wide, narrow, narrow, wide, narrow, narrow)],
        scratch_shapes=low(wide, narrow, narrow) + number(ids)
        + low(wide, narrow, narrow) + number(ids) + low(wide, wide, wide)
        + number(ids, ids) + low(narrow, narrow, narrow, wide, packed, packed, packed, packed, diags, diags, diags, diags, narrow)
        + [pltpu.VMEM(diags, F32)]
        + [pltpu.SemaphoreType.DMA((n,)) for n in (9, 12 + kv_local, 12 + kv_local, splits, splits, splits * kv_local, splits * kv_local)],
        compiler_params=pltpu.CompilerParams(
            collective_id=0, has_side_effects=True, vmem_limit_bytes=60 * 2**20
        ),
        cost_estimate=pl.CostEstimate(flops=2**30, bytes_accessed=2**23, transcendentals=2**20),
    )(
        fwd_q[0], fwd_k[0], fwd_v[0], fwd_segments, held_q[0], held_k[0], held_v[0], back_segments, up_grad[0]
    )
    results = pl.pallas_call(
        write_all,
        in_specs=[anywhere] * 7,
        out_specs=[pl.BlockSpec(memory_space=pltpu.HBM)] * 7,
        out_shape=[jax.ShapeDtypeStruct(result.shape, LOW) for result in results],
        scratch_shapes=[pltpu.VMEM(result.shape, LOW) for result in results] + [pltpu.SemaphoreType.DMA((7,))] * 2,
        compiler_params=pltpu.CompilerParams(vmem_limit_bytes=60 * 2**20),
    )(*results)
    return tuple(result[None] for result in results)


def solution(mesh):
    heads = P("section", None, "tp")
    tokens = P("section", None)
    return jax.shard_map(
        shards,
        mesh=mesh,
        in_specs=(heads, heads, heads, tokens, heads, heads, heads, tokens, heads),
        out_specs=(P("section", "tp", None),) + (heads,) * 6,
        check_vma=False,
    )
```

```python
import functools

import jax
import jax.numpy as jnp
from jax import lax
from jax.experimental import pallas as pl
from jax.experimental.pallas import tpu as pltpu
from jax.sharding import PartitionSpec as P

HQ = 64
KV = 8
HD = 128
GROUP = HQ // KV
PARTS = 4
SCALE = HD**-0.5
LOW = jnp.bfloat16
F32 = jnp.float32
MESH = pl.DeviceIdType.MESH


def dot_nt(a, b):
    return lax.dot_general(a, b, (((1,), (1,)), ((), ())), preferred_element_type=F32)


def dot_tn(a, b):
    return lax.dot_general(a, b, (((0,), (0,)), ((), ())), preferred_element_type=F32)


def dot_nn(a, b):
    return lax.dot_general(a, b, (((1,), (0,)), ((), ())), preferred_element_type=F32)


def iotas(shape):
    return lax.broadcasted_iota(jnp.int32, shape, 0), lax.broadcasted_iota(jnp.int32, shape, 1)


def segment_sides(ids_ref):
    tokens = ids_ref.shape[1]
    across = jnp.broadcast_to(ids_ref[...].astype(F32), (tokens, tokens))
    return across.T, across


def allowed_mask(down, across):
    rows, cols = iotas(down.shape)
    return (down == across) & (cols <= rows)


def probability(q, k, allowed):
    scores = jnp.where(allowed, dot_nt(q, k) * SCALE, -jnp.inf)
    weights = jnp.exp(scores - jnp.max(scores, axis=1, keepdims=True))
    return weights / jnp.sum(weights, axis=1, keepdims=True)


def pack(full):
    half = full.shape[0] // 2
    rows, cols = iotas((half, half))
    turned = full[half:, :].T
    packed = full[:half, :half] + turned[:half] + jnp.where(rows < cols, turned[half:], 0.0)
    diag = jnp.sum(jnp.where(rows == cols, full[half:, half:], 0.0), axis=0, keepdims=True)
    return packed, diag


def unpack_masks(down, across):
    half = down.shape[0] // 2
    rows, cols = iotas((half, half))
    first = (down[:half, :half] == across[:half, :half]) & (cols <= rows)
    cross = down[:half, :half] == across[:half, half:]
    second = (down[half:, half:] == across[half:, half:]) & (rows < cols)
    return first, jnp.concatenate([cross, second], axis=0), rows == cols


def unpack(packed, diag, masks):
    first, turned_mask, eye = masks
    turned = jnp.where(turned_mask, jnp.concatenate([packed, packed], axis=0), 0.0).T
    half = packed.shape[0]
    zero = jnp.zeros((half, half), F32)
    on_diag = jnp.where(eye, jnp.broadcast_to(diag, (half, half)), 0.0)
    top = jnp.concatenate([jnp.where(first, packed, 0.0), zero], axis=1)
    bottom = turned + jnp.concatenate([zero, on_diag], axis=1)
    return jnp.concatenate([top, bottom], axis=0)


def diag_rows(kv_local, tokens):
    rows = kv_local * GROUP * (tokens // 2) // HD
    return -(-rows // 16) * 16


def store_packed(g, parts, diag_scratch, pack_ref):
    half = parts[0][0].shape[0]
    values = jnp.concatenate([p for p, _ in parts], axis=1).astype(LOW)
    pack_ref[pl.ds(pl.multiple_of(g * half, half), half), :] = values
    diags = jnp.concatenate([d for _, d in parts], axis=1)
    rows, _ = iotas(diag_scratch.shape)
    merged = diag_scratch[...]
    lines = diags.shape[1] // HD
    for c in range(lines):
        line = jnp.broadcast_to(diags[:, c * HD : (c + 1) * HD], rows.shape)
        merged = jnp.where(rows == g * lines + c, line, merged)
    diag_scratch[...] = merged


def load_packed(g, pack_ref, diag_ref):
    half = pack_ref.shape[1] // GROUP
    values = pack_ref[pl.ds(pl.multiple_of(g * half, half), half), :].astype(F32)
    tail = diag_ref[...].astype(F32)
    rows, _ = iotas(tail.shape)
    lines = pack_ref.shape[1] // HD
    found = [jnp.sum(jnp.where(rows == g * lines + c, tail, 0.0), axis=0, keepdims=True) for c in range(lines)]
    diags = jnp.concatenate(found, axis=1)
    return [
        (values[:, h * half : (h + 1) * half], diags[:, h * half : (h + 1) * half]) for h in range(GROUP)
    ]


def head(g, h):
    return pl.ds(pl.multiple_of((g * GROUP + h) * HD, HD), HD)


def own(g):
    return pl.ds(pl.multiple_of(g * HD, HD), HD)


def score_gradient(prob, grad, v):
    dprob = dot_nt(grad, v)
    delta = jnp.sum(prob * dprob, axis=1, keepdims=True)
    return prob * (dprob - delta) * SCALE


def every_group(kv_local, body):
    lax.fori_loop(0, kv_local, lambda g, carry: (body(g), carry)[1], 0)


def tick(
    sections, splits,
    fwd_q, fwd_k, fwd_v, fwd_ids, held_q, held_k, held_v, back_ids, up_grad,
    passed, evicted_q, evicted_k, evicted_v, grad_q, grad_k, grad_v,
    fq, fk, fv, fids, hq, hk, hv, bids, ug,
    out, near, holder_ids, far_ids, keys, third, third_in, arriving, pack_out, pack_in, score_out, score_in, pack_dout, pack_din, score_dout, score_din, gk, diag,
    load_sem, send_sem, recv_sem, out_send, out_recv, near_send, near_recv,
):
    me, lane = lax.axis_index("section"), lax.axis_index("tp")
    mirror = sections - 1 - me
    right, left = lax.rem(me + 1, sections), lax.rem(me + sections - 1, sections)
    section_short = right == mirror
    holder_short = lax.rem(mirror + 1, sections) == me
    tokens = hq.shape[0]
    kv_local = hk.shape[1] // HD
    rows = tokens // splits
    width = hq.shape[1]

    pairs = [(held_q, hq), (held_k, hk), (held_v, hv), (up_grad, ug), (fwd_q, fq), (fwd_k, fk), (fwd_v, fv),
             (fwd_ids, fids), (back_ids, bids)]
    loads = [pltpu.make_async_copy(src, dst, load_sem.at[n]) for n, (src, dst) in enumerate(pairs)]
    for load in loads:
        load.start()

    barrier = pltpu.get_barrier_semaphore()
    pl.semaphore_signal(barrier, inc=1, device_id=(mirror, lane), device_id_type=MESH)
    for t in range(splits):
        pl.semaphore_signal(barrier, inc=1, device_id=(left, t), device_id_type=MESH)
        pl.semaphore_signal(barrier, inc=1, device_id=(right, t), device_id_type=MESH)
    for t in range(1, splits):
        peer = lax.rem(lane + t, splits)
        pl.semaphore_signal(barrier, inc=1, device_id=(me, peer), device_id_type=MESH)
    pl.semaphore_wait(barrier, 3 * splits)

    def remote(n, src, dst, section):
        return pltpu.make_async_remote_copy(
            src_ref=src, dst_ref=dst, send_sem=send_sem.at[n], recv_sem=recv_sem.at[n],
            device_id=(section, lane), device_id_type=MESH,
        )


    def block(g, base=0):
        return pl.ds(pl.multiple_of(base + g * GROUP * HD, GROUP * HD), GROUP * HD)

    send_ids = remote(0, back_ids, holder_ids, mirror)
    send_keys = remote(1, held_k, keys, mirror)
    send_ek = remote(2, fwd_k, evicted_k, mirror)
    send_ev = remote(3, fwd_v, evicted_v, mirror)
    send_pack = remote(4, pack_out, pack_in, mirror)
    send_third = remote(5, third, third_in, mirror)
    send_score = remote(6, score_out, score_in, mirror)
    send_gk = remote(7, gk, grad_k, mirror)
    send_up = remote(8, up_grad, arriving, left)
    send_pack_diag = remote(9, pack_dout, pack_din, mirror)
    send_score_diag = remote(10, score_dout, score_din, mirror)
    send_eq = [remote(12 + g, fwd_q.at[:, block(g)], evicted_q.at[:, block(g)], mirror) for g in range(kv_local)]
    early = (kv_local + 1) // 2
    send_far = remote(11, fwd_ids, far_ids, mirror)
    send_out = []
    for offset in range(splits):
        to = lax.rem(lane + offset, splits)
        send_out.append(
            pltpu.make_async_remote_copy(
                src_ref=out.at[pl.ds(pl.multiple_of(to * rows, rows), rows)],
                dst_ref=passed.at[:, pl.ds(pl.multiple_of(lane * width, width), width)],
                send_sem=out_send.at[offset], recv_sem=out_recv.at[offset],
                device_id=(right, to), device_id_type=MESH,
            )
        )

    def near_copies(g):
        copies = []
        for offset in range(splits):
            to = lax.rem(lane + offset, splits)
            src = near.at[pl.ds(pl.multiple_of(to * rows, rows), rows), block(g)]
            dst = passed.at[:, block(g, lane * width)]
            n = offset * kv_local + g
            if offset == 0:
                copies.append(pltpu.make_async_copy(src, dst, near_send.at[n]))
            else:
                copies.append(
                    pltpu.make_async_remote_copy(
                        src_ref=src, dst_ref=dst, send_sem=near_send.at[n], recv_sem=near_recv.at[n],
                        device_id=(me, to), device_id_type=MESH,
                    )
                )
        return copies

    send_ids.start()
    send_far.start()
    send_keys.start()
    send_ek.start()
    send_ev.start()

    @pl.when(jnp.logical_not(holder_short))
    def _():
        send_up.start()

    diag[...] = jnp.zeros(diag.shape, F32)

    for load in loads[:4]:
        load.wait()
    send_ids.wait_recv()

    @pl.when(jnp.logical_not(holder_short))
    def _():
        allowed = allowed_mask(*segment_sides(holder_ids))

        def group(g):
            k = hk[:, own(g)]
            parts = [pack(probability(hq[:, head(g, h)], k, allowed)) for h in range(GROUP)]
            store_packed(g, parts, diag, pack_out)

        every_group(kv_local, group)
        third[...] = hv[...]

    @pl.when(holder_short)
    def _():
        allowed = allowed_mask(*segment_sides(holder_ids))

        def group(g):
            k, v = hk[:, own(g)], hv[:, own(g)]
            total = jnp.zeros((tokens, HD), F32)
            parts = []
            for h in range(GROUP):
                prob = probability(hq[:, head(g, h)], k, allowed)
                grad = ug[:, head(g, h)]
                total = total + dot_tn(prob.astype(LOW), grad)
                parts.append(pack(score_gradient(prob, grad, v)))
            store_packed(g, parts, diag, pack_out)
            third[:, own(g)] = total.astype(LOW)

        every_group(kv_local, group)

    pack_dout[...] = diag[...].astype(LOW)
    send_pack.start()
    send_pack_diag.start()
    send_third.start()
    for send in send_eq[:early]:
        send.start()

    @pl.when(jnp.logical_or(section_short, holder_short))
    def _():
        for send in send_eq[early:]:
            send.start()

    def key_gradient(ref, diag_ref):
        holder_masks = unpack_masks(*segment_sides(holder_ids))

        def group(g):
            total = jnp.zeros((tokens, HD), F32)
            for h, (packed, on_diag) in enumerate(load_packed(g, ref, diag_ref)):
                dscore = unpack(packed, on_diag, holder_masks).astype(LOW)
                total = total + dot_tn(dscore, hq[:, head(g, h)])
            gk[:, own(g)] = total.astype(LOW)

        every_group(kv_local, group)

    @pl.when(holder_short)
    def _():
        key_gradient(pack_out, pack_dout)
        send_gk.start()

    for load in loads[4:]:
        load.wait()

    def forward_group(allowed, out_ref, g):
        k, v = fk[:, own(g)], fv[:, own(g)]
        for h in range(GROUP):
            prob = probability(fq[:, head(g, h)], k, allowed)
            out_ref[:, head(g, h)] = dot_nn(prob.astype(LOW), v).astype(LOW)

    @pl.when(jnp.logical_not(section_short))
    def _():
        every_group(kv_local, functools.partial(forward_group, allowed_mask(*segment_sides(fids)), out))
        for send in send_out:
            send.start()

    send_keys.wait_recv()
    send_pack.wait_recv()
    send_pack_diag.wait_recv()
    send_third.wait_recv()
    masks = unpack_masks(*segment_sides(bids))

    @pl.when(jnp.logical_not(section_short))
    def _():
        send_up.wait_recv()

        def group(g):
            k, v = keys[:, own(g)], third_in[:, own(g)]
            total = jnp.zeros((tokens, HD), F32)
            parts = []
            for h, (packed, on_diag) in enumerate(load_packed(g, pack_in, pack_din)):
                prob = unpack(packed, on_diag, masks)
                grad = arriving[:, head(g, h)]
                total = total + dot_tn(prob.astype(LOW), grad)
                dscore = score_gradient(prob, grad, v)
                grad_q[:, head(g, h)] = dot_nn(dscore.astype(LOW), k).astype(LOW)
                parts.append(pack(dscore))
            store_packed(g, parts, diag, score_out)
            grad_v[:, own(g)] = total.astype(LOW)

        every_group(kv_local, group)
        score_dout[...] = diag[...].astype(LOW)
        send_score.start()
        send_score_diag.start()

        @pl.when(jnp.logical_not(holder_short))
        def _():
            for send in send_eq[early:]:
                send.start()


    @pl.when(section_short)
    def _():
        def group(g):
            k = keys[:, own(g)]
            for h, (packed, on_diag) in enumerate(load_packed(g, pack_in, pack_din)):
                dscore = unpack(packed, on_diag, masks)
                grad_q[:, head(g, h)] = dot_nn(dscore.astype(LOW), k).astype(LOW)

        every_group(kv_local, group)
        grad_v[...] = third_in[...]

    @pl.when(jnp.logical_not(holder_short))
    def _():
        send_score.wait_recv()
        send_score_diag.wait_recv()
        key_gradient(score_in, score_din)
        send_gk.start()


    for send in [send_ek, send_ev, send_far]:
        send.wait_recv()

    @pl.when(holder_short)
    def _():
        again = [
            pltpu.make_async_copy(src, dst, load_sem.at[4 + n])
            for n, (src, dst) in enumerate([(evicted_k, fk), (evicted_v, fv)])
        ]
        for load in again:
            load.start()
        for load in again:
            load.wait()
        allowed = allowed_mask(*segment_sides(far_ids))
        for g in range(kv_local):
            send_eq[g].wait_recv()
            load = pltpu.make_async_copy(evicted_q.at[:, block(g)], fq.at[:, block(g)], load_sem.at[6])
            load.start()
            load.wait()
            forward_group(allowed, near, g)
            for copy in near_copies(g):
                copy.start()
        for g in range(kv_local):
            for copy in near_copies(g):
                copy.wait()

    @pl.when(jnp.logical_not(holder_short))
    def _():
        for send in send_eq:
            send.wait_recv()

    @pl.when(jnp.logical_not(holder_short))
    def _():
        for send in send_out:
            send.wait_recv()

    for send in [send_ids, send_far, send_keys, send_ek, send_ev, send_pack, send_pack_diag, send_third, send_gk] + send_eq:
        send.wait_send()

    @pl.when(jnp.logical_not(holder_short))
    def _():
        send_up.wait_send()

    @pl.when(jnp.logical_not(section_short))
    def _():
        send_score.wait_send()
        send_score_diag.wait_send()
        for send in send_out:
            send.wait_send()

    send_gk.wait_recv()


def write_all(*refs):
    count = (len(refs) - 2) // 3
    here, there, rooms = refs[:count], refs[count : 2 * count], refs[2 * count : 3 * count]
    in_sem, out_sem = refs[3 * count :]
    parts = []
    for n in range(count):
        step = here[n].shape[0] // PARTS if here[n].shape[0] % (16 * PARTS) == 0 else here[n].shape[0]
        parts += [(n, pl.ds(at, step), at // step) for at in range(0, here[n].shape[0], step)]
    reads = [pltpu.make_async_copy(here[n].at[r], rooms[n].at[r], in_sem.at[n, p]) for n, r, p in parts]
    writes = [pltpu.make_async_copy(rooms[n].at[r], there[n].at[r], out_sem.at[n, p]) for n, r, p in parts]
    for read in reads:
        read.start()
    for read, write in zip(reads, writes):
        read.wait()
        write.start()
    for write in writes:
        write.wait()


def shards(fwd_q, fwd_k, fwd_v, fwd_segments, held_q, held_k, held_v, back_segments, up_grad):
    sections, splits = lax.axis_size("section"), lax.axis_size("tp")
    tokens, width = held_q.shape[1], held_q.shape[2]
    narrow_width = held_k.shape[2]
    kv_local = narrow_width // HD
    wide, narrow, ids = (tokens, width), (tokens, narrow_width), (1, tokens)
    packed = (kv_local * (tokens // 2), GROUP * (tokens // 2))
    diags = (diag_rows(kv_local, tokens), HD)
    passed = (tokens // splits, splits * width)
    anywhere, vmem = pl.BlockSpec(memory_space=pl.ANY), pl.BlockSpec(memory_space=pltpu.VMEM)

    def low(*shapes):
        return [pltpu.VMEM(shape, LOW) for shape in shapes]

    def number(*shapes):
        return [pltpu.VMEM(shape, jnp.int32) for shape in shapes]

    results = pl.pallas_call(
        functools.partial(tick, sections, splits),
        in_specs=[pl.BlockSpec(memory_space=pltpu.HBM)] * 9,
        out_specs=[anywhere] * 4 + [vmem, anywhere, vmem],
        out_shape=[jax.ShapeDtypeStruct(s, LOW) for s in (passed, wide, narrow, narrow, wide, narrow, narrow)],
        scratch_shapes=low(wide, narrow, narrow) + number(ids)
        + low(wide, narrow, narrow) + number(ids) + low(wide, wide, wide)
        + number(ids, ids) + low(narrow, narrow, narrow, wide, packed, packed, packed, packed, diags, diags, diags, diags, narrow)
        + [pltpu.VMEM(diags, F32)]
        + [pltpu.SemaphoreType.DMA((n,)) for n in (9, 12 + kv_local, 12 + kv_local, splits, splits, splits * kv_local, splits * kv_local)],
        compiler_params=pltpu.CompilerParams(
            collective_id=0, has_side_effects=True, vmem_limit_bytes=60 * 2**20
        ),
        cost_estimate=pl.CostEstimate(flops=2**30, bytes_accessed=2**23, transcendentals=2**20),
    )(
        fwd_q[0], fwd_k[0], fwd_v[0], fwd_segments, held_q[0], held_k[0], held_v[0], back_segments, up_grad[0]
    )
    results = pl.pallas_call(
        write_all,
        in_specs=[anywhere] * 7,
        out_specs=[pl.BlockSpec(memory_space=pltpu.HBM)] * 7,
        out_shape=[jax.ShapeDtypeStruct(result.shape, LOW) for result in results],
        scratch_shapes=[pltpu.VMEM(result.shape, LOW) for result in results] + [pltpu.SemaphoreType.DMA((7, PARTS))] * 2,
        compiler_params=pltpu.CompilerParams(vmem_limit_bytes=60 * 2**20),
    )(*results)
    return tuple(result[None] for result in results)


def solution(mesh):
    heads = P("section", None, "tp")
    tokens = P("section", None)
    return jax.shard_map(
        shards,
        mesh=mesh,
        in_specs=(heads, heads, heads, tokens, heads, heads, heads, tokens, heads),
        out_specs=(P("section", "tp", None),) + (heads,) * 6,
        check_vma=False,
    )
```
